32 devices in a mesh: dp: 2 (over core), row: 4 (over y, x), col: 4 (over z).
Axes of the slice: x: 2, y: 2, z: 4, core: 2. Of those that a mesh axis runs over, the one named last changes fastest.
Arguments:
- hidden_in: bfloat16 [4096, 576], P(('dp', 'col', 'row')), may hold values from -6 to 6
- cotangent: bfloat16 [4096, 576], P(('dp', 'col', 'row'))
- lengths: int32 [8], P(('dp', 'col')), may hold values from 1 to 512, as said below
- gains: float32 [2, 2, 576], replicated, may hold values from 0.5 to 1.5
- w_qkv: bfloat16 [2, 576, 960], P(None, 'col', 'row'), may hold values from -0.25 to 0.25
- w_out: bfloat16 [2, 576, 576], P(None, 'row', 'col'), may hold values from -1.5 to 1.5
- w_gate: bfloat16 [2, 576, 1536], P(None, 'col', 'row'), may hold values from -0.25 to 0.25
- w_up: bfloat16 [2, 576, 1536], P(None, 'col', 'row'), may hold values from -0.25 to 0.25
- w_down: bfloat16 [2, 1536, 576], P(None, 'row', 'col'), may hold values from -0.15625 to 0.15625
Outputs:
- hidden_out: bfloat16 [4096, 576], P(('dp', 'col', 'row'))
- grad_hidden: float32 [4096, 576], P(('dp', 'col', 'row'))
- grad_gains: float32 [2, 2, 576], replicated
- grad_qkv: float32 [2, 576, 960], P(None, 'col', 'row')
- grad_out: float32 [2, 576, 576], P(None, 'row', 'col')
- grad_gate: float32 [2, 576, 1536], P(None, 'col', 'row')
- grad_up: float32 [2, 576, 1536], P(None, 'col', 'row')
- grad_down: float32 [2, 1536, 576], P(None, 'row', 'col')
The draws below stay inside these ranges and needn't reach their ends.
Inputs may be any that keep to these rules, and one draw needn't show every extreme that they name: Pack p holds one sequence of lengths[p] tokens at its start; the rest of the pack is padding. Some pack holds exactly 512 tokens.
All inputs are finite; a program needn't handle non-finite values.
Results may differ from the reference program's by a relative error of at most 0.03.
Values may be sent and summed in bfloat16 or wider, within the bound.
No kernel may reach another device: no remote copies, remote signals or barrier semaphores. Data moves between devices by JAX's collectives and lax.ppermute only.
A program may use at most 128 MiB of HBM per device.

```python
import jax
import jax.numpy as jnp
from jax import lax

D = 576
HEADS = 9
KV_HEADS = 3
HEAD_DIM = 64
FF = 1536
LAYERS = 2
QKV = 960
PACK = 512
PACKS = 8
TOKENS = 4096


def draw_lengths(key, part):
    key = jax.random.fold_in(key, 11)
    first_key, second_key = jax.random.split(key)
    drawn = jax.random.randint(first_key, (PACKS,), 1, PACK + 1)
    chosen = jax.random.randint(second_key, (), 0, PACKS)
    drawn = jnp.where(jnp.arange(PACKS) == chosen, PACK, drawn)
    return drawn.astype(jnp.int32)


def draw_cotangent(key, part):
    key = jax.random.fold_in(key, 5)
    rising = jnp.exp(jnp.log(3.0) * jnp.arange(TOKENS).astype(jnp.float32) / TOKENS)[:, None]
    base_vals = jax.random.normal(key, (TOKENS, D), jnp.float32)
    return (base_vals * rising).astype(jnp.bfloat16)


def levels(own_key, shape, cuts, low, top_value):
    factor_of, own = 1.0, jax.random.fold_in(own_key, 6)
    for axis_at, parts in cuts:
        draws = jnp.exp(jax.random.uniform(jax.random.fold_in(own, axis_at), (parts,), jnp.float32, low / len(cuts), top_value / len(cuts)))
        factor_of = factor_of * jnp.repeat(draws, shape[axis_at] // parts).reshape([-1 if axis == axis_at else 1 for axis in range(len(shape))])
    return factor_of


def normal_values(own_key, shape, deviation, limit, cuts=(), kind=jnp.bfloat16):
    result = jax.random.normal(own_key, shape, jnp.float32) * deviation
    if len(cuts) > 0:
        result = levels(own_key, shape, cuts, -0.22, 0.18) * result
    return jnp.clip(result, min=-limit, max=limit).astype(kind)


def setup_inputs(seed: int = 0) -> dict:
    splits = jax.random.split(jax.random.key(seed), 10)
    hidden_in = normal_values(splits[0], (TOKENS, D), 1.0, 6.0, ((0, 32),))
    cotangent = draw_cotangent(jax.random.fold_in(splits[9], 71), 0)
    lengths = draw_lengths(jax.random.fold_in(splits[9], 71), 0)
    gains = jnp.clip(1.0 + 0.1 * jax.random.normal(splits[3], (LAYERS, 2, D), jnp.float32), 0.5, 1.5)
    w_qkv = normal_values(splits[4], (LAYERS, D, QKV), D ** -0.5, 0.25, ((1, 4), (2, 4)))
    w_out = normal_values(splits[5], (LAYERS, D, D), (D // 32) ** -0.5, 1.5, ((1, 4), (2, 4)))
    w_gate = normal_values(splits[6], (LAYERS, D, FF), D ** -0.5, 0.25, ((1, 4), (2, 4)))
    w_up = normal_values(splits[7], (LAYERS, D, FF), D ** -0.5, 0.25, ((1, 4), (2, 4)))
    w_down = normal_values(splits[8], (LAYERS, FF, D), FF ** -0.5, 0.15625, ((1, 4), (2, 4)))
    return {"hidden_in": hidden_in, "cotangent": cotangent, "lengths": lengths, "gains": gains, "w_qkv": w_qkv, "w_out": w_out, "w_gate": w_gate, "w_up": w_up, "w_down": w_down}


@jax.custom_vjp
def low(v):
    return lax.optimization_barrier(v.astype(jnp.bfloat16)).astype(jnp.float32)

@jax.custom_vjp
def low_back(v):
    return v

def low_keep(v):
    return (low(v), None)

def low_pass(kept, grad):
    return (grad,)

def back_keep(v):
    return (v, None)

def back_low(kept, grad):
    return (low(grad),)
low.defvjp(low_keep, low_pass)
low_back.defvjp(back_keep, back_low)
eps_norm = 1e-05
rope_base = 100000.0
masked_score = -1e+30

def matmul(left, right):
    return jnp.dot(left, right, precision=lax.Precision.HIGHEST, preferred_element_type=jnp.float32)

def rms_norm(resid, gain):
    return resid * lax.rsqrt(lax.optimization_barrier(jnp.mean(resid * resid, -1, keepdims=True)) + eps_norm) * gain

def rope_tables(first_place, amount):
    half_dim = HEAD_DIM // 2
    places = (first_place + jnp.arange(amount)).astype(jnp.float32)
    frequency = rope_base ** (-(2.0 * jnp.arange(half_dim).astype(jnp.float32)) / HEAD_DIM)
    angles = places[:, None] * frequency[None, :]
    return (jnp.cos(angles)[:, None, :], jnp.sin(angles)[:, None, :])

def rotate(values, cosine, sine_vals):
    half_dim = values.shape[-1] // 2
    first_half = values[..., :half_dim]
    second_half = values[..., half_dim:]
    return jnp.concatenate([first_half * cosine - second_half * sine_vals, second_half * cosine + first_half * sine_vals], -1)

def attend(inputs):
    query, keys_rot, values, length = inputs
    group_size = HEADS // KV_HEADS
    grouped = query.reshape(PACK, KV_HEADS, group_size, HEAD_DIM)
    scores = jnp.einsum('qghd,kgd->ghqk', grouped, keys_rot, precision=lax.Precision.HIGHEST) * HEAD_DIM ** (-0.5)
    scores = low_back(scores)
    places = jnp.arange(PACK)
    visible = (places[None, :] <= places[:, None]) & (places[None, :] < length)
    scores = jnp.where(visible, scores, masked_score)
    top_score = lax.optimization_barrier(jnp.max(scores, -1, keepdims=True))
    raw_weights = jnp.exp(scores - top_score)
    probs = raw_weights / lax.optimization_barrier(jnp.sum(raw_weights, -1, keepdims=True))
    output = jnp.einsum('ghqk,kgd->qghd', low(probs), values, precision=lax.Precision.HIGHEST)
    return output.reshape(PACK, D)

def forward(resid, gain_vals, w_query, w_attend, w_gating, w_upward, w_downward, lengths):
    kv_width = KV_HEADS * HEAD_DIM
    cosine, sine_vals = rope_tables(0, PACK)
    for layer in range(LAYERS):
        normed = low(rms_norm(resid, gain_vals[layer, 0]))
        mixed = low(low_back(matmul(normed, w_query[layer]))).reshape(PACKS, PACK, QKV)
        query = mixed[:, :, :D].reshape(PACKS, PACK, HEADS, HEAD_DIM)
        keys_raw = mixed[:, :, D:D + kv_width].reshape(PACKS, PACK, KV_HEADS, HEAD_DIM)
        values = mixed[:, :, D + kv_width:].reshape(PACKS, PACK, KV_HEADS, HEAD_DIM)
        query = low(rotate(query, cosine, sine_vals))
        keys_rot = low(rotate(keys_raw, cosine, sine_vals))
        attended = lax.map(jax.checkpoint(attend), (query, keys_rot, values, lengths))
        attended = low(low_back(attended.reshape(TOKENS, D)))
        resid = resid + low_back(matmul(attended, w_attend[layer]))
        normed = low(rms_norm(resid, gain_vals[layer, 1]))
        gate_act = low_back(matmul(normed, w_gating[layer]))
        up_act = low_back(matmul(normed, w_upward[layer]))
        hidden = low(gate_act * jax.nn.sigmoid(gate_act) * up_act)
        resid = resid + low_back(matmul(hidden, w_downward[layer]))
    return resid

def reference(hidden_in, cotangent, lengths, gains, w_qkv, w_out, w_gate, w_up, w_down):

    def run(resid, gain_vals, w_query, w_attend, w_gating, w_upward, w_downward):
        return forward(resid, gain_vals, w_query, w_attend, w_gating, w_upward, w_downward, lengths)
    output, pullback = jax.vjp(run, hidden_in.astype(jnp.float32), gains.astype(jnp.float32), w_qkv.astype(jnp.float32), w_out.astype(jnp.float32), w_gate.astype(jnp.float32), w_up.astype(jnp.float32), w_down.astype(jnp.float32))
    grads = pullback(cotangent.astype(jnp.float32))
    return (output.astype(jnp.bfloat16), grads[0], grads[1], grads[2], grads[3], grads[4], grads[5], grads[6])
```

```python
import jax
import jax.numpy as jnp
from jax import lax
from jax.sharding import PartitionSpec as P

D = 576
HEADS = 9
KV_HEADS = 3
HEAD_DIM = 64
GROUP = HEADS // KV_HEADS
KV = KV_HEADS * HEAD_DIM
QKV = D + 2 * KV

eps_norm = 1e-05
rope_base = 100000.0
masked_score = -1e30
bf16 = jnp.bfloat16
f32 = jnp.float32


def mm(spec, left, right):
    return jnp.einsum(spec, left, right, preferred_element_type=f32)


def rope_tables(first_place, amount):
    half_dim = HEAD_DIM // 2
    places = (first_place + jnp.arange(amount)).astype(f32)
    frequency = rope_base ** (-(2.0 * jnp.arange(half_dim).astype(f32)) / HEAD_DIM)
    angles = places[:, None] * frequency[None, :]
    return (jnp.cos(angles)[:, None, :], jnp.sin(angles)[:, None, :])


def rotate(values, cosine, sine_vals):
    half_dim = values.shape[-1] // 2
    first_half = values[..., :half_dim]
    second_half = values[..., half_dim:]
    return jnp.concatenate(
        [
            first_half * cosine - second_half * sine_vals,
            second_half * cosine + first_half * sine_vals,
        ],
        -1,
    )


def norm_back(resid, inverse, gain, grad_norm):
    scaled = resid * inverse
    weighted = grad_norm * gain
    return inverse * (weighted - scaled * jnp.mean(weighted * scaled, -1, keepdims=True))


def swap(values, axis, bit):
    return lax.ppermute(values, axis, [(i, i ^ bit) for i in range(lax.axis_size(axis))])


def spread(values, axes, amount):
    copies = jnp.broadcast_to(values[None], (amount,) + values.shape)
    return lax.all_to_all(copies, axes, 0, 0, tiled=True)


def merge_halves(own, other, core):
    low = jnp.where(core == 0, own, other)
    high = jnp.where(core == 0, other, own)
    return jnp.stack([low, high], -3)


def sum_pairs(values):
    size = lax.axis_size("dp")
    total = values.astype(f32)
    for step in range(2, size, 2):
        moved = lax.ppermute(values, "dp", [(i, (i + step) % size) for i in range(size)])
        total = total + moved.astype(f32)
    return total.astype(values.dtype)


def halve(values, core):
    axis = values.ndim - 3
    keep = lax.dynamic_index_in_dim(values, core, axis, keepdims=False)
    send = lax.dynamic_index_in_dim(values, 1 - core, axis, keepdims=False)
    return sum_pairs((keep.astype(f32) + swap(send, "dp", 1).astype(f32)).astype(bf16))


def on_device(hidden_in, cotangent, lengths, gains, w_qkv, w_out, w_gate, w_up, w_down):
    rows = hidden_in.shape[0]
    size_row = lax.axis_size("row")
    size_col = lax.axis_size("col")
    core = lax.axis_index("dp") % 2
    first_place = lax.axis_index("row") * rows
    pack = rows * size_row
    length = lengths[0]
    layers, deep, wide_qkv = w_qkv.shape
    wide_out = w_out.shape[1]
    wide = w_gate.shape[2]
    half = deep // 2
    score_scale = HEAD_DIM ** (-0.5)

    out_flip = jnp.swapaxes(w_out, 1, 2)
    down_flip = jnp.swapaxes(w_down, 1, 2)
    attn_blocks = jnp.concatenate([w_qkv, out_flip], -1)
    full_qkv, full_out, full_gate, full_up, full_down = [], [], [], [], []
    for layer in range(layers):
        mine = lax.dynamic_slice_in_dim(attn_blocks[layer], core * half, half, 0)
        part = spread(mine, ("row", "col"), size_row * size_col)
        part = part.reshape(size_row, size_col, half, wide_qkv + wide_out)
        whole = merge_halves(part, swap(part, "dp", 1), core)
        whole = whole.reshape(size_row, D, wide_qkv + wide_out)
        full_qkv.append(whole[:, :, :wide_qkv])
        full_out.append(whole[:, :, wide_qkv:])
        feed = jnp.stack([w_gate[layer], w_up[layer], down_flip[layer]], 0)
        mine = lax.dynamic_slice_in_dim(feed, core * half, half, 1)
        part = spread(mine, "col", size_col)
        part = jnp.stack([part, swap(part, "row", 2)], 0)
        part = jnp.transpose(part, (2, 0, 1, 3, 4))
        part = part.reshape(3, 2, size_col, half, wide)
        whole = merge_halves(part, swap(part, "dp", 1), core).reshape(3, 2, D, wide)
        full_gate.append(whole[0])
        full_up.append(whole[1])
        full_down.append(whole[2])

    cosine, sine_vals = rope_tables(0, pack)
    own_cosine, own_sine = rope_tables(first_place, rows)
    key_places = jnp.arange(pack)
    query_places = first_place + jnp.arange(rows)
    visible = (key_places[None, :] <= query_places[:, None]) & (key_places[None, :] < length)

    def own_rows(values):
        return lax.dynamic_slice_in_dim(values, first_place, rows, 0)

    resid = hidden_in.astype(f32)
    both_cotangent = jnp.concatenate([cotangent, swap(cotangent, "row", 1)], 0)
    stored = []
    for layer in range(layers):
        if layer == 0:
            resid_all = lax.all_gather(hidden_in, "row", axis=0, tiled=True).astype(f32)
            inverse_all = lax.rsqrt(jnp.mean(resid_all * resid_all, -1, keepdims=True) + eps_norm)
            scaled_all = resid_all * inverse_all
            normed_all = (scaled_all * gains[layer, 0]).astype(bf16)
            inverse1 = own_rows(inverse_all)
        else:
            inverse1 = lax.rsqrt(jnp.mean(resid * resid, -1, keepdims=True) + eps_norm)
            normed1 = (resid * inverse1 * gains[layer, 0]).astype(bf16)
            normed_all = lax.all_gather(normed1, "row", axis=0, tiled=True)
        mixed = mm("td,rdk->trk", normed_all, full_qkv[layer]).astype(bf16).reshape(pack, QKV)
        query = own_rows(mixed[:, :D]).astype(f32).reshape(rows, HEADS, HEAD_DIM)
        query_rot = rotate(query, own_cosine, own_sine).astype(bf16)
        query_rot = query_rot.reshape(rows, KV_HEADS, GROUP, HEAD_DIM)
        keys = mixed[:, D : D + KV].astype(f32).reshape(pack, KV_HEADS, HEAD_DIM)
        keys_rot = rotate(keys, cosine, sine_vals).astype(bf16)
        values = mixed[:, D + KV :].reshape(pack, KV_HEADS, HEAD_DIM)
        scores = mm("qghd,kgd->ghqk", query_rot, keys_rot) * score_scale
        scores = jnp.where(visible, scores, masked_score)
        top_score = jnp.max(scores, -1, keepdims=True)
        raw_weights = jnp.exp(scores - top_score)
        probs = raw_weights / jnp.sum(raw_weights, -1, keepdims=True)
        attended = mm("ghqk,kgd->qghd", probs.astype(bf16), values)
        attended = attended.reshape(rows, D).astype(bf16)
        attended_blocks = attended.reshape(rows, size_row, wide_out)
        resid_mid = resid + mm("trk,rdk->td", attended_blocks, full_out[layer])
        inverse2 = lax.rsqrt(jnp.mean(resid_mid * resid_mid, -1, keepdims=True) + eps_norm)
        normed2 = (resid_mid * inverse2 * gains[layer, 1]).astype(bf16)
        both_normed2 = jnp.concatenate([normed2, swap(normed2, "row", 1)], 0)
        gate_act = mm("td,bdf->tbf", both_normed2, full_gate[layer])
        up_act = mm("td,bdf->tbf", both_normed2, full_up[layer])
        hidden = (gate_act * jax.nn.sigmoid(gate_act) * up_act).astype(bf16)
        down_part = mm("tbf,bdf->td", hidden, full_down[layer])
        moved = swap(down_part[rows:].astype(bf16), "row", 1).astype(f32)
        resid_next = resid_mid + down_part[:rows] + moved
        stored.append(
            (
                resid,
                inverse1,
                normed_all,
                query_rot,
                keys_rot,
                values,
                probs,
                attended_blocks,
                resid_mid,
                inverse2,
                both_normed2,
                gate_act,
                up_act,
                hidden,
            )
        )
        resid = resid_next

    grad_resid = cotangent.astype(f32)
    attn_grads = [None] * layers
    feed_grads = [None] * layers
    gain_grads = [None] * layers
    for layer in reversed(range(layers)):
        (
            resid_in,
            inverse1,
            normed_all,
            query_rot,
            keys_rot,
            values,
            probs,
            attended_blocks,
            resid_mid,
            inverse2,
            both_normed2,
            gate_act,
            up_act,
            hidden,
        ) = stored[layer]
        if layer == layers - 1:
            both_grad = both_cotangent
        else:
            grad_low = grad_resid.astype(bf16)
            both_grad = jnp.concatenate([grad_low, swap(grad_low, "row", 1)], 0)
        grad_hid = mm("td,bdf->tbf", both_grad, full_down[layer])
        sigma = jax.nn.sigmoid(gate_act)
        grad_gate_act = (grad_hid * up_act * sigma * (1.0 + gate_act * (1.0 - sigma))).astype(bf16)
        grad_up_act = (grad_hid * gate_act * sigma).astype(bf16)
        norm2_part = mm("tbf,bdf->td", grad_gate_act, full_gate[layer])
        norm2_part = norm2_part + mm("tbf,bdf->td", grad_up_act, full_up[layer])
        moved = swap(norm2_part[rows:].astype(bf16), "row", 1).astype(f32)
        grad_norm2 = norm2_part[:rows] + moved
        feed_grad = jnp.stack(
            [
                mm("td,tbf->bdf", both_normed2, grad_gate_act).astype(bf16),
                mm("td,tbf->bdf", both_normed2, grad_up_act).astype(bf16),
                mm("td,tbf->bdf", both_grad, hidden).astype(bf16),
            ],
            1,
        )
        feed_grad = halve(feed_grad.reshape(2, 3, size_col, 2, half, wide), core)
        feed_grad = feed_grad[0].astype(f32) + swap(feed_grad[1], "row", 2).astype(f32)
        feed_grad = jnp.swapaxes(feed_grad.astype(bf16), 0, 1)
        feed_grad = lax.all_to_all(feed_grad, "col", 0, 0, tiled=True)
        feed_grad = jnp.sum(feed_grad.astype(f32), 0)
        other = swap(feed_grad, "dp", 1)
        feed_grads[layer] = merge_halves(feed_grad, other, core).reshape(3, deep, wide)

        gain_grad2 = jnp.sum(grad_norm2 * (resid_mid * inverse2), 0)
        grad_resid = grad_resid + norm_back(resid_mid, inverse2, gains[layer, 1], grad_norm2)
        grad_low = grad_resid.astype(bf16)
        grad_att = mm("td,rdk->trk", grad_low, full_out[layer]).astype(bf16)
        grad_att = grad_att.reshape(rows, KV_HEADS, GROUP, HEAD_DIM)
        grad_out = mm("td,trk->rdk", grad_low, attended_blocks).astype(bf16)
        grad_probs = mm("qghd,kgd->ghqk", grad_att, values)
        row_dots = jnp.sum(grad_probs * probs, -1, keepdims=True)
        grad_scores = (probs * (grad_probs - row_dots)).astype(bf16)
        grad_query = mm("ghqk,kgd->qghd", grad_scores, keys_rot) * score_scale
        grad_keys = mm("ghqk,qghd->kgd", grad_scores, query_rot) * score_scale
        grad_values = mm("ghqk,qghd->kgd", probs.astype(bf16), grad_att)
        grad_query = rotate(grad_query.reshape(rows, HEADS, HEAD_DIM), own_cosine, -own_sine)
        grad_keys = rotate(grad_keys, cosine, -sine_vals)
        grad_query = grad_query.reshape(rows, D).astype(bf16)
        grad_query = lax.dynamic_update_slice_in_dim(
            jnp.zeros((pack, D), bf16), grad_query, first_place, 0
        )
        grad_mixed = jnp.concatenate(
            [
                grad_query,
                grad_keys.reshape(pack, KV).astype(bf16),
                grad_values.reshape(pack, KV).astype(bf16),
            ],
            -1,
        ).reshape(pack, size_row, wide_qkv)
        norm1_part = mm("trk,rdk->td", grad_mixed, full_qkv[layer])
        grad_norm1 = lax.all_to_all(
            norm1_part.astype(bf16).reshape(size_row, rows, D), "row", 0, 0, tiled=True
        )
        grad_norm1 = jnp.sum(grad_norm1.astype(f32), 0)
        if layer == 0:
            gain_grad1 = jnp.sum(norm1_part * scaled_all, 0)
        else:
            gain_grad1 = jnp.sum(grad_norm1 * (resid_in * inverse1), 0)
        grad_resid = grad_resid + norm_back(resid_in, inverse1, gains[layer, 0], grad_norm1)
        gain_grads[layer] = jnp.stack([gain_grad1, gain_grad2], 0)
        grad_qkv = mm("td,trk->rdk", normed_all, grad_mixed).astype(bf16)
        attn_grad = jnp.concatenate([grad_qkv, grad_out], -1)
        attn_grad = attn_grad.reshape(size_row, size_col, 2, half, wide_qkv + wide_out)
        attn_grad = halve(attn_grad, core)
        blocks = size_row * size_col
        attn_grad = attn_grad.reshape(blocks, half, wide_qkv + wide_out)
        if layer == 0:
            gain_part = jnp.stack(gain_grads, 0)
            gain_part = sum_pairs((gain_part + swap(gain_part, "dp", 1)).astype(bf16))
            gain_rows = gain_part.reshape(-1, wide_qkv + wide_out)
            extra = gain_rows.shape[0]
            gain_rows = jnp.pad(gain_rows, ((0, -extra % 8), (0, 0)))
            gain_rows = jnp.broadcast_to(gain_rows[None], (blocks,) + gain_rows.shape)
            attn_grad = jnp.concatenate([attn_grad, gain_rows], 1)
        attn_grad = lax.all_to_all(attn_grad, ("row", "col"), 0, 0, tiled=True)
        attn_grad = jnp.sum(attn_grad.astype(f32), 0)
        if layer == 0:
            gain_total = attn_grad[half : half + extra].reshape(layers, 2, D)
            attn_grad = attn_grad[:half]
        other = swap(attn_grad, "dp", 1)
        attn_grads[layer] = merge_halves(attn_grad, other, core).reshape(deep, -1)

    attn_grads = jnp.stack(attn_grads, 0)
    feed_grads = jnp.stack(feed_grads, 0)
    return (
        resid.astype(bf16),
        grad_resid,
        gain_total,
        attn_grads[:, :, :wide_qkv],
        jnp.swapaxes(attn_grads[:, :, wide_qkv:], 1, 2),
        feed_grads[:, 0],
        feed_grads[:, 1],
        jnp.swapaxes(feed_grads[:, 2], 1, 2),
    )


def solution(mesh):
    tokens = P(("dp", "col", "row"), None)
    return jax.shard_map(
        on_device,
        mesh=mesh,
        in_specs=(
            tokens,
            tokens,
            P(("dp", "col")),
            P(),
            P(None, "col", "row"),
            P(None, "row", "col"),
            P(None, "col", "row"),
            P(None, "col", "row"),
            P(None, "row", "col"),
        ),
        out_specs=(
            tokens,
            tokens,
            P(),
            P(None, "col", "row"),
            P(None, "row", "col"),
            P(None, "col", "row"),
            P(None, "col", "row"),
            P(None, "row", "col"),
        ),
        check_vma=False,
    )
```

```python
import jax
import jax.numpy as jnp
from jax import lax
from jax.sharding import PartitionSpec as P

D = 576
HEADS = 9
KV_HEADS = 3
HEAD_DIM = 64
GROUP = HEADS // KV_HEADS
KV = KV_HEADS * HEAD_DIM
QKV = D + 2 * KV

eps_norm = 1e-05
rope_base = 100000.0
masked_score = -1e30
bf16 = jnp.bfloat16
f32 = jnp.float32


def mm(spec, left, right):
    return jnp.einsum(spec, left, right, preferred_element_type=f32)


def rope_tables(first_place, amount):
    half_dim = HEAD_DIM // 2
    places = (first_place + jnp.arange(amount)).astype(f32)
    frequency = rope_base ** (-(2.0 * jnp.arange(half_dim).astype(f32)) / HEAD_DIM)
    angles = places[:, None] * frequency[None, :]
    return (jnp.cos(angles)[:, None, :], jnp.sin(angles)[:, None, :])


def rotate(values, cosine, sine_vals):
    half_dim = values.shape[-1] // 2
    first_half = values[..., :half_dim]
    second_half = values[..., half_dim:]
    return jnp.concatenate(
        [
            first_half * cosine - second_half * sine_vals,
            second_half * cosine + first_half * sine_vals,
        ],
        -1,
    )


def norm_back(resid, inverse, gain, grad_norm):
    scaled = resid * inverse
    weighted = grad_norm * gain
    return inverse * (weighted - scaled * jnp.mean(weighted * scaled, -1, keepdims=True))


def swap(values, axis, bit):
    return lax.ppermute(values, axis, [(i, i ^ bit) for i in range(lax.axis_size(axis))])


def spread(values, axis):
    copies = jnp.broadcast_to(values[None], (lax.axis_size(axis),) + values.shape)
    return lax.all_to_all(copies, axis, 0, 0, tiled=True)


def scatter_sum(values, axis):
    place = lax.axis_index(axis)
    total = lax.dynamic_index_in_dim(values, place, 0, keepdims=False).astype(f32)
    for bits in range(1, lax.axis_size(axis)):
        send = lax.dynamic_index_in_dim(values, place ^ bits, 0, keepdims=False)
        total = total + swap(send, axis, bits).astype(f32)
    return total


def after(values, *earlier):
    return lax.optimization_barrier((values,) + earlier)[0]


def merge_halves(own, other, core):
    low = jnp.where(core == 0, own, other)
    high = jnp.where(core == 0, other, own)
    return jnp.stack([low, high], -3)


def sum_pairs(values):
    size = lax.axis_size("dp")
    total = values.astype(f32)
    for step in range(2, size, 2):
        moved = lax.ppermute(values, "dp", [(i, (i + step) % size) for i in range(size)])
        total = total + moved.astype(f32)
    return total.astype(values.dtype)


def halve(values, core):
    axis = values.ndim - 3
    keep = lax.dynamic_index_in_dim(values, core, axis, keepdims=False)
    send = lax.dynamic_index_in_dim(values, 1 - core, axis, keepdims=False)
    return sum_pairs((keep.astype(f32) + swap(send, "dp", 1).astype(f32)).astype(bf16))


def on_device(hidden_in, cotangent, lengths, gains, w_qkv, w_out, w_gate, w_up, w_down):
    rows = hidden_in.shape[0]
    size_row = lax.axis_size("row")
    size_col = lax.axis_size("col")
    core = lax.axis_index("dp") % 2
    first_place = lax.axis_index("row") * rows
    pack = rows * size_row
    length = lengths[0]
    layers, deep, wide_qkv = w_qkv.shape
    wide_out = w_out.shape[1]
    wide = w_gate.shape[2]
    half = deep // 2
    score_scale = HEAD_DIM ** (-0.5)

    both = wide_qkv + wide_out
    attn_blocks = jnp.concatenate([w_qkv, jnp.swapaxes(w_out, 1, 2)], -1)
    attn_half = lax.dynamic_slice_in_dim(attn_blocks, core * half, half, 1)
    feed_blocks = jnp.stack([w_gate, w_up, jnp.swapaxes(w_down, 1, 2)], 1)
    feed_half = lax.dynamic_slice_in_dim(feed_blocks, core * half, half, 2)
    full_attn, full_gate, full_up, full_down = [], [], [], []
    part = None
    for layer in range(layers):
        mine = attn_half[layer] if part is None else after(attn_half[layer], part)
        part = spread(spread(mine, "col"), "row")
        whole = merge_halves(part, swap(part, "dp", 1), core)
        full_attn.append(whole.reshape(size_row, D, both))
    feed_parts = lax.all_gather(feed_half, "col", axis=2)
    for layer in range(layers):
        part = feed_parts[layer]
        part = jnp.stack([part, swap(part, "row", 2)], 1)
        whole = merge_halves(part, swap(part, "dp", 1), core).reshape(3, 2, D, wide)
        full_gate.append(whole[0])
        full_up.append(whole[1])
        full_down.append(whole[2])

    cosine, sine_vals = rope_tables(0, pack)
    own_cosine, own_sine = rope_tables(first_place, rows)
    key_places = jnp.arange(pack)
    query_places = first_place + jnp.arange(rows)
    visible = (key_places[None, :] <= query_places[:, None]) & (key_places[None, :] < length)

    def own_rows(values):
        return lax.dynamic_slice_in_dim(values, first_place, rows, 0)

    resid = hidden_in.astype(f32)
    both_cotangent = jnp.concatenate([cotangent, swap(cotangent, "row", 1)], 0)
    stored = []
    for layer in range(layers):
        if layer == 0:
            resid_all = lax.all_gather(hidden_in, "row", axis=0, tiled=True).astype(f32)
            inverse_all = lax.rsqrt(jnp.mean(resid_all * resid_all, -1, keepdims=True) + eps_norm)
            scaled_all = resid_all * inverse_all
            normed_all = (scaled_all * gains[layer, 0]).astype(bf16)
            inverse1 = own_rows(inverse_all)
        else:
            inverse1 = lax.rsqrt(jnp.mean(resid * resid, -1, keepdims=True) + eps_norm)
            normed1 = (resid * inverse1 * gains[layer, 0]).astype(bf16)
            normed_all = lax.all_gather(normed1, "row", axis=0, tiled=True)
        mixed = mm("td,rdk->trk", normed_all, full_attn[layer])[:, :, :wide_qkv]
        mixed = mixed.astype(bf16).reshape(pack, QKV)
        query = own_rows(mixed[:, :D]).astype(f32).reshape(rows, HEADS, HEAD_DIM)
        query_rot = rotate(query, own_cosine, own_sine).astype(bf16)
        query_rot = query_rot.reshape(rows, KV_HEADS, GROUP, HEAD_DIM)
        keys = mixed[:, D : D + KV].astype(f32).reshape(pack, KV_HEADS, HEAD_DIM)
        keys_rot = rotate(keys, cosine, sine_vals).astype(bf16)
        values = mixed[:, D + KV :].reshape(pack, KV_HEADS, HEAD_DIM)
        scores = mm("qghd,kgd->ghqk", query_rot, keys_rot) * score_scale
        scores = jnp.where(visible, scores, masked_score)
        top_score = jnp.max(scores, -1, keepdims=True)
        raw_weights = jnp.exp(scores - top_score)
        probs = raw_weights / jnp.sum(raw_weights, -1, keepdims=True)
        attended = mm("ghqk,kgd->qghd", probs.astype(bf16), values)
        attended = attended.reshape(rows, D).astype(bf16)
        attended_blocks = attended.reshape(rows, size_row, wide_out)
        attended_blocks = jnp.pad(attended_blocks, ((0, 0), (0, 0), (wide_qkv, 0)))
        resid_mid = resid + mm("trk,rdk->td", attended_blocks, full_attn[layer])
        inverse2 = lax.rsqrt(jnp.mean(resid_mid * resid_mid, -1, keepdims=True) + eps_norm)
        normed2 = (resid_mid * inverse2 * gains[layer, 1]).astype(bf16)
        both_normed2 = jnp.concatenate([normed2, swap(normed2, "row", 1)], 0)
        gate_act = mm("td,bdf->tbf", both_normed2, full_gate[layer])
        up_act = mm("td,bdf->tbf", both_normed2, full_up[layer])
        hidden = (gate_act * jax.nn.sigmoid(gate_act) * up_act).astype(bf16)
        down_part = mm("tbf,bdf->td", hidden, full_down[layer])
        moved = swap(down_part[rows:].astype(bf16), "row", 1).astype(f32)
        resid_next = resid_mid + down_part[:rows] + moved
        stored.append(
            (
                resid,
                inverse1,
                normed_all,
                query_rot,
                keys_rot,
                values,
                probs,
                attended_blocks,
                resid_mid,
                inverse2,
                both_normed2,
                gate_act,
                up_act,
                hidden,
            )
        )
        resid = resid_next

    grad_resid = cotangent.astype(f32)
    attn_grads = [None] * layers
    feed_grads = [None] * layers
    gain_grads = [None] * layers
    waiting = {}
    for layer in reversed(range(layers)):
        (
            resid_in,
            inverse1,
            normed_all,
            query_rot,
            keys_rot,
            values,
            probs,
            attended_blocks,
            resid_mid,
            inverse2,
            both_normed2,
            gate_act,
            up_act,
            hidden,
        ) = stored[layer]
        if layer == layers - 1:
            both_grad = both_cotangent
        else:
            grad_low = grad_resid.astype(bf16)
            both_grad = jnp.concatenate([grad_low, swap(grad_low, "row", 1)], 0)
            both_grad = after(both_grad, waiting["feed_two"])
        grad_hid = mm("td,bdf->tbf", both_grad, full_down[layer])
        sigma = jax.nn.sigmoid(gate_act)
        grad_gate_act = (grad_hid * up_act * sigma * (1.0 + gate_act * (1.0 - sigma))).astype(bf16)
        grad_up_act = (grad_hid * gate_act * sigma).astype(bf16)
        norm2_part = mm("tbf,bdf->td", grad_gate_act, full_gate[layer])
        norm2_part = norm2_part + mm("tbf,bdf->td", grad_up_act, full_up[layer])
        moved = norm2_part[rows:].astype(bf16)
        if waiting:
            moved = after(moved, waiting["attn_half"])
        moved = swap(moved, "row", 1).astype(f32)
        grad_norm2 = norm2_part[:rows] + moved
        feed_grad = jnp.stack(
            [
                mm("td,tbf->bdf", both_normed2, grad_gate_act).astype(bf16),
                mm("td,tbf->bdf", both_normed2, grad_up_act).astype(bf16),
                mm("td,tbf->bdf", both_grad, hidden).astype(bf16),
            ],
            1,
        )
        feed_half_sum = halve(feed_grad.reshape(2, 3, size_col, 2, half, wide), core)
        feed_two = feed_half_sum[0].astype(f32) + swap(feed_half_sum[1], "row", 2).astype(f32)
        feed_two = jnp.swapaxes(feed_two.astype(bf16), 0, 1)
        feed_grad = scatter_sum(feed_two, "col")
        other = swap(feed_grad, "dp", 1)
        feed_grads[layer] = merge_halves(feed_grad, other, core).reshape(3, deep, wide)

        gain_grad2 = jnp.sum(grad_norm2 * (resid_mid * inverse2), 0)
        grad_resid = grad_resid + norm_back(resid_mid, inverse2, gains[layer, 1], grad_norm2)
        grad_low = grad_resid.astype(bf16)
        if waiting:
            grad_low = after(grad_low, waiting["feed_grad"])
        grad_att = mm("td,rdk->trk", grad_low, full_attn[layer])[:, :, wide_qkv:].astype(bf16)
        grad_att = grad_att.reshape(rows, KV_HEADS, GROUP, HEAD_DIM)
        grad_out = mm("td,trk->rdk", grad_low, attended_blocks)
        grad_probs = mm("qghd,kgd->ghqk", grad_att, values)
        row_dots = jnp.sum(grad_probs * probs, -1, keepdims=True)
        grad_scores = (probs * (grad_probs - row_dots)).astype(bf16)
        grad_query = mm("ghqk,kgd->qghd", grad_scores, keys_rot) * score_scale
        grad_keys = mm("ghqk,qghd->kgd", grad_scores, query_rot) * score_scale
        grad_values = mm("ghqk,qghd->kgd", probs.astype(bf16), grad_att)
        grad_query = rotate(grad_query.reshape(rows, HEADS, HEAD_DIM), own_cosine, -own_sine)
        grad_keys = rotate(grad_keys, cosine, -sine_vals)
        grad_query = grad_query.reshape(rows, D).astype(bf16)
        grad_query = lax.dynamic_update_slice_in_dim(
            jnp.zeros((pack, D), bf16), grad_query, first_place, 0
        )
        grad_mixed = jnp.concatenate(
            [
                grad_query,
                grad_keys.reshape(pack, KV).astype(bf16),
                grad_values.reshape(pack, KV).astype(bf16),
            ],
            -1,
        ).reshape(pack, size_row, wide_qkv)
        grad_mixed = jnp.pad(grad_mixed, ((0, 0), (0, 0), (0, wide_out)))
        grad_mixed = after(grad_mixed, feed_half_sum)
        if waiting:
            grad_mixed = after(grad_mixed, waiting["attn_row"])
        norm1_part = mm("trk,rdk->td", grad_mixed, full_attn[layer])
        norm1_blocks = norm1_part.astype(bf16).reshape(size_row, rows, D)
        if layer == 0:
            grad_norm1 = scatter_sum(norm1_blocks, "row")
        else:
            grad_norm1 = lax.all_to_all(norm1_blocks, "row", 0, 0, tiled=True)
            grad_norm1 = jnp.sum(grad_norm1.astype(f32), 0)
        if layer == 0:
            gain_grad1 = jnp.sum(norm1_part * scaled_all, 0)
        else:
            gain_grad1 = jnp.sum(grad_norm1 * (resid_in * inverse1), 0)
        grad_resid = grad_resid + norm_back(resid_in, inverse1, gains[layer, 0], grad_norm1)
        gain_grads[layer] = jnp.stack([gain_grad1, gain_grad2], 0)
        attn_grad = (mm("td,trk->rdk", normed_all, grad_mixed) + grad_out).astype(bf16)
        attn_grad = halve(attn_grad.reshape(size_row, size_col, 2, half, both), core)
        if layer == 0:
            gain_part = jnp.stack(gain_grads, 0)
            gain_part = sum_pairs((gain_part + swap(gain_part, "dp", 1)).astype(bf16))
            gain_rows = gain_part.reshape(-1, both)
            extra = gain_rows.shape[0]
            gain_rows = jnp.pad(gain_rows, ((0, -extra % 8), (0, 0)))
            gain_rows = jnp.broadcast_to(gain_rows, (size_row, size_col) + gain_rows.shape)
            attn_grad = jnp.concatenate([attn_grad, gain_rows], 2)
        waiting = {"feed_two": feed_two, "feed_grad": feed_grad, "attn_half": attn_grad}
        attn_grad = lax.all_to_all(attn_grad, "row", 0, 0, tiled=True)
        attn_grad = jnp.sum(attn_grad.astype(f32), 0).astype(bf16)
        waiting["attn_row"] = attn_grad
        attn_grad = lax.all_to_all(attn_grad, "col", 0, 0, tiled=True)
        attn_grad = jnp.sum(attn_grad.astype(f32), 0)
        if layer == 0:
            gain_total = attn_grad[half : half + extra].reshape(layers, 2, D)
            attn_grad = attn_grad[:half]
        other = swap(attn_grad, "dp", 1)
        attn_grads[layer] = merge_halves(attn_grad, other, core).reshape(deep, -1)

    attn_grads = jnp.stack(attn_grads, 0)
    feed_grads = jnp.stack(feed_grads, 0)
    return (
        resid.astype(bf16),
        grad_resid,
        gain_total,
        attn_grads[:, :, :wide_qkv],
        jnp.swapaxes(attn_grads[:, :, wide_qkv:], 1, 2),
        feed_grads[:, 0],
        feed_grads[:, 1],
        jnp.swapaxes(feed_grads[:, 2], 1, 2),
    )


def solution(mesh):
    tokens = P(("dp", "col", "row"), None)
    return jax.shard_map(
        on_device,
        mesh=mesh,
        in_specs=(
            tokens,
            tokens,
            P(("dp", "col")),
            P(),
            P(None, "col", "row"),
            P(None, "row", "col"),
            P(None, "col", "row"),
            P(None, "col", "row"),
            P(None, "row", "col"),
        ),
        out_specs=(
            tokens,
            tokens,
            P(),
            P(None, "col", "row"),
            P(None, "row", "col"),
            P(None, "col", "row"),
            P(None, "col", "row"),
            P(None, "row", "col"),
        ),
        check_vma=False,
    )
```

```python
import jax
import jax.numpy as jnp
from jax import lax
from jax.sharding import PartitionSpec as P

D = 576
HEADS = 9
KV_HEADS = 3
HEAD_DIM = 64
GROUP = HEADS // KV_HEADS
KV = KV_HEADS * HEAD_DIM
QKV = D + 2 * KV

eps_norm = 1e-05
rope_base = 100000.0
masked_score = -1e30
bf16 = jnp.bfloat16
f32 = jnp.float32


def mm(spec, left, right):
    return jnp.einsum(spec, left, right, preferred_element_type=f32)


def rope_tables(token_places):
    half_dim = HEAD_DIM // 2
    places = token_places.astype(f32)
    frequency = rope_base ** (-(2.0 * jnp.arange(half_dim).astype(f32)) / HEAD_DIM)
    angles = places[:, None] * frequency[None, :]
    return (jnp.cos(angles)[:, None, :], jnp.sin(angles)[:, None, :])


def rotate(values, cosine, sine_vals):
    half_dim = values.shape[-1] // 2
    first_half = values[..., :half_dim]
    second_half = values[..., half_dim:]
    return jnp.concatenate(
        [
            first_half * cosine - second_half * sine_vals,
            second_half * cosine + first_half * sine_vals,
        ],
        -1,
    )


def norm_back(resid, inverse, gain, grad_norm):
    scaled = resid * inverse
    weighted = grad_norm * gain
    return inverse * (weighted - scaled * jnp.mean(weighted * scaled, -1, keepdims=True))


def swap(values, axis, bit):
    return lax.ppermute(values, axis, [(i, i ^ bit) for i in range(lax.axis_size(axis))])


def neighbours(values, axis):
    return [values] + [swap(values, axis, bits) for bits in range(1, lax.axis_size(axis))]


def in_order(blocks, axis):
    place = lax.axis_index(axis)
    held = jnp.stack(blocks, 0)
    return jnp.stack(
        [
            lax.dynamic_index_in_dim(held, place ^ index, 0, keepdims=False)
            for index in range(len(blocks))
        ],
        0,
    )


def spread(values, axis):
    size = lax.axis_size(axis)
    copies = jnp.broadcast_to(values[None], (size,) + values.shape)
    return lax.all_to_all(copies, axis, 0, 0, tiled=True)


def feed_whole(block, core, size_row, size_col):
    halves = block.reshape(3, 2, block.shape[1] // 2, block.shape[2])
    mine = lax.dynamic_index_in_dim(halves, core, 1, keepdims=False)
    size = lax.axis_size("dp")
    groups = [
        [
            ((2 * pair + data) * size_row + high * 2 + low) * size_col + column
            for high in range(2)
            for column in range(size_col)
            for data in range(2)
        ]
        for pair in range(size // 2)
        for low in range(2)
    ]
    whole = lax.all_gather(mine, ("dp", "row", "col"), axis=0, axis_index_groups=groups)
    return whole.reshape((2, size_col, 2) + mine.shape)


def exchange_sum(values, axes):
    return jnp.sum(lax.all_to_all(values, axes, 0, 0, tiled=True).astype(f32), 0)


def scatter_sum(values, axis):
    place = lax.axis_index(axis)
    total = lax.dynamic_index_in_dim(values, place, 0, keepdims=False).astype(f32)
    for bits in range(1, lax.axis_size(axis)):
        send = lax.dynamic_index_in_dim(values, place ^ bits, 0, keepdims=False)
        total = total + swap(send, axis, bits).astype(f32)
    return total


def after(values, *earlier):
    zero = 0.0
    for array in earlier:
        first = array[(0,) * array.ndim].astype(f32)
        zero = zero + jnp.minimum(jnp.abs(first), 0.0)
    return values + zero.astype(values.dtype)


def merge_halves(own, other, core):
    low = jnp.where(core == 0, own, other)
    high = jnp.where(core == 0, other, own)
    return jnp.stack([low, high], -3)


def joined(part, core):
    whole = merge_halves(part, swap(part, "dp", 1), core)
    return whole.reshape(whole.shape[0], -1, whole.shape[-1])


def sum_pairs(values):
    size = lax.axis_size("dp")
    total = values.astype(f32)
    for step in range(2, size, 2):
        moved = lax.ppermute(values, "dp", [(i, (i + step) % size) for i in range(size)])
        total = total + moved.astype(f32)
    return total.astype(values.dtype)


def halve(values, core):
    axis = values.ndim - 3
    keep = lax.dynamic_index_in_dim(values, core, axis, keepdims=False)
    send = lax.dynamic_index_in_dim(values, 1 - core, axis, keepdims=False)
    return sum_pairs((keep.astype(f32) + swap(send, "dp", 1).astype(f32)).astype(bf16))


def on_device(hidden_in, cotangent, lengths, gains, w_qkv, w_out, w_gate, w_up, w_down):
    rows = hidden_in.shape[0]
    size_row = lax.axis_size("row")
    size_col = lax.axis_size("col")
    core = lax.axis_index("dp") % 2
    pack = rows * size_row
    length = lengths[0]
    layers, deep, wide_qkv = w_qkv.shape
    wide_out = w_out.shape[1]
    wide = w_gate.shape[2]
    half = deep // 2
    score_scale = HEAD_DIM ** (-0.5)

    both = wide_qkv + wide_out
    attn_blocks = jnp.concatenate([w_qkv, jnp.swapaxes(w_out, 1, 2)], -1)
    attn_half = lax.dynamic_slice_in_dim(attn_blocks, core * half, half, 1)
    feed_blocks = jnp.stack([w_gate, w_up, jnp.swapaxes(w_down, 1, 2)], 1)
    hidden_blocks = neighbours(hidden_in, "row")
    attn_cols = in_order(neighbours(attn_half, "col"), "col")
    full_attn, feed_parts = [], []
    for layer in range(layers):
        if layer == 0:
            part = spread(after(attn_cols[:, layer], *hidden_blocks[1:]), "row")
            full_attn.append(joined(part, core))
        else:
            full_attn.append(spread(after(attn_cols[:, layer], full_attn[0]), "row"))
        feed_parts.append(feed_whole(feed_blocks[layer], core, size_row, size_col))
    full_gate, full_up, full_down = [], [], []

    place = lax.axis_index("row")
    key_places = jnp.concatenate(
        [(place ^ bits) * rows + jnp.arange(rows) for bits in range(size_row)], 0
    )
    cosine, sine_vals = rope_tables(key_places)
    own_cosine, own_sine = cosine[:rows], sine_vals[:rows]
    query_places = key_places[:rows]
    visible = (key_places[None, :] <= query_places[:, None]) & (key_places[None, :] < length)

    resid = hidden_in.astype(f32)
    late_cotangent = after(cotangent, full_attn[0])
    both_cotangent = jnp.concatenate([cotangent, swap(late_cotangent, "row", 1)], 0)
    stored = []
    for layer in range(layers):
        if layer == 0:
            resid_all = jnp.concatenate(hidden_blocks, 0).astype(f32)
            inverse_all = lax.rsqrt(jnp.mean(resid_all * resid_all, -1, keepdims=True) + eps_norm)
            scaled_all = resid_all * inverse_all
            normed_all = (scaled_all * gains[layer, 0]).astype(bf16)
            inverse1 = inverse_all[:rows]
        else:
            inverse1 = lax.rsqrt(jnp.mean(resid * resid, -1, keepdims=True) + eps_norm)
            normed1 = (resid * inverse1 * gains[layer, 0]).astype(bf16)
            normed_all = jnp.concatenate(neighbours(normed1, "row"), 0)
        mixed = mm("td,rdk->trk", normed_all, full_attn[layer])[:, :, :wide_qkv]
        mixed = mixed.astype(bf16).reshape(pack, QKV)
        query = mixed[:rows, :D].astype(f32).reshape(rows, HEADS, HEAD_DIM)
        query_rot = rotate(query, own_cosine, own_sine).astype(bf16)
        query_rot = query_rot.reshape(rows, KV_HEADS, GROUP, HEAD_DIM)
        keys = mixed[:, D : D + KV].astype(f32).reshape(pack, KV_HEADS, HEAD_DIM)
        keys_rot = rotate(keys, cosine, sine_vals).astype(bf16)
        values = mixed[:, D + KV :].reshape(pack, KV_HEADS, HEAD_DIM)
        scores = mm("qghd,kgd->ghqk", query_rot, keys_rot) * score_scale
        scores = jnp.where(visible, scores, masked_score)
        top_score = jnp.max(scores, -1, keepdims=True)
        raw_weights = jnp.exp(scores - top_score)
        probs = raw_weights / jnp.sum(raw_weights, -1, keepdims=True)
        attended = mm("ghqk,kgd->qghd", probs.astype(bf16), values)
        attended = attended.reshape(rows, D).astype(bf16)
        attended_blocks = attended.reshape(rows, size_row, wide_out)
        attended_blocks = jnp.pad(attended_blocks, ((0, 0), (0, 0), (wide_qkv, 0)))
        resid_mid = resid + mm("trk,rdk->td", attended_blocks, full_attn[layer])
        inverse2 = lax.rsqrt(jnp.mean(resid_mid * resid_mid, -1, keepdims=True) + eps_norm)
        normed2 = (resid_mid * inverse2 * gains[layer, 1]).astype(bf16)
        both_normed2 = jnp.concatenate([normed2, swap(normed2, "row", 1)], 0)
        feed = after(feed_parts[layer], normed2)
        full_gate.append(feed[:, :, :, 0].reshape(2, D, wide))
        full_up.append(feed[:, :, :, 1].reshape(2, D, wide))
        full_down.append(feed[:, :, :, 2].reshape(2, D, wide))
        if layer + 1 < layers:
            full_attn[layer + 1] = joined(after(full_attn[layer + 1], normed2), core)
        gate_act = mm("td,bdf->tbf", both_normed2, full_gate[layer])
        up_act = mm("td,bdf->tbf", both_normed2, full_up[layer])
        hidden = (gate_act * jax.nn.sigmoid(gate_act) * up_act).astype(bf16)
        down_part = mm("tbf,bdf->td", hidden, full_down[layer])
        moved = swap(down_part[rows:].astype(bf16), "row", 1).astype(f32)
        resid_next = resid_mid + down_part[:rows] + moved
        stored.append(
            (
                resid,
                inverse1,
                normed_all,
                query_rot,
                keys_rot,
                values,
                probs,
                attended_blocks,
                resid_mid,
                inverse2,
                both_normed2,
                gate_act,
                up_act,
                hidden,
            )
        )
        resid = resid_next

    grad_resid = cotangent.astype(f32)
    attn_grads = [None] * layers
    feed_grads = [None] * layers
    gain_grads = [None] * layers
    for layer in reversed(range(layers)):
        (
            resid_in,
            inverse1,
            normed_all,
            query_rot,
            keys_rot,
            values,
            probs,
            attended_blocks,
            resid_mid,
            inverse2,
            both_normed2,
            gate_act,
            up_act,
            hidden,
        ) = stored[layer]
        if layer == layers - 1:
            both_grad = both_cotangent
        else:
            grad_low = grad_resid.astype(bf16)
            both_grad = jnp.concatenate([grad_low, swap(grad_low, "row", 1)], 0)
        grad_hid = mm("td,bdf->tbf", both_grad, full_down[layer])
        sigma = jax.nn.sigmoid(gate_act)
        grad_gate_act = (grad_hid * up_act * sigma * (1.0 + gate_act * (1.0 - sigma))).astype(bf16)
        grad_up_act = (grad_hid * gate_act * sigma).astype(bf16)
        norm2_part = mm("tbf,bdf->td", grad_gate_act, full_gate[layer])
        norm2_part = norm2_part + mm("tbf,bdf->td", grad_up_act, full_up[layer])
        moved = swap(norm2_part[rows:].astype(bf16), "row", 1).astype(f32)
        grad_norm2 = norm2_part[:rows] + moved
        feed_grad = jnp.stack(
            [
                mm("td,tbf->bdf", both_normed2, grad_gate_act).astype(bf16),
                mm("td,tbf->bdf", both_normed2, grad_up_act).astype(bf16),
                mm("td,tbf->bdf", both_grad, hidden).astype(bf16),
            ],
            1,
        )
        feed_half_sum = halve(feed_grad.reshape(2, 3, size_col, 2, half, wide), core)
        keep = lax.dynamic_index_in_dim(feed_half_sum, place // 2, 0, keepdims=False)
        send = lax.dynamic_index_in_dim(feed_half_sum, 1 - place // 2, 0, keepdims=False)
        feed_two = keep.astype(f32) + swap(send, "row", 2).astype(f32)
        feed_two = jnp.swapaxes(feed_two, 0, 1).astype(bf16).reshape(-1, wide)
        feed_grad = lax.psum_scatter(feed_two, "col", scatter_dimension=0, tiled=True)
        feed_grads[layer] = feed_grad.reshape(3, half, wide)

        gain_grad2 = jnp.sum(grad_norm2 * (resid_mid * inverse2), 0)
        grad_resid = grad_resid + norm_back(resid_mid, inverse2, gains[layer, 1], grad_norm2)
        grad_low = after(grad_resid, feed_half_sum).astype(bf16)
        grad_att = mm("td,rdk->trk", grad_low, full_attn[layer])[:, :, wide_qkv:].astype(bf16)
        grad_att = grad_att.reshape(rows, KV_HEADS, GROUP, HEAD_DIM)
        grad_out = mm("td,trk->rdk", grad_low, attended_blocks)
        grad_probs = mm("qghd,kgd->ghqk", grad_att, values)
        row_dots = jnp.sum(grad_probs * probs, -1, keepdims=True)
        grad_scores = (probs * (grad_probs - row_dots)).astype(bf16)
        grad_query = mm("ghqk,kgd->qghd", grad_scores, keys_rot) * score_scale
        grad_keys = mm("ghqk,qghd->kgd", grad_scores, query_rot) * score_scale
        grad_values = mm("ghqk,qghd->kgd", probs.astype(bf16), grad_att)
        grad_query = rotate(grad_query.reshape(rows, HEADS, HEAD_DIM), own_cosine, -own_sine)
        grad_keys = rotate(grad_keys, cosine, -sine_vals)
        grad_query = grad_query.reshape(rows, D).astype(bf16)
        grad_query = jnp.pad(grad_query, ((0, pack - rows), (0, 0)))
        grad_mixed = jnp.concatenate(
            [
                grad_query,
                grad_keys.reshape(pack, KV).astype(bf16),
                grad_values.reshape(pack, KV).astype(bf16),
            ],
            -1,
        ).reshape(pack, size_row, wide_qkv)
        grad_mixed = jnp.pad(grad_mixed, ((0, 0), (0, 0), (0, wide_out)))
        norm1_part = mm("trk,rdk->td", grad_mixed, full_attn[layer])
        grad_norm1 = norm1_part[:rows]
        norm1_low = norm1_part.astype(bf16)
        for bits in range(1, size_row):
            moved = swap(norm1_low[bits * rows : (bits + 1) * rows], "row", bits)
            grad_norm1 = grad_norm1 + moved.astype(f32)
        if layer == 0:
            gain_grad1 = jnp.sum(norm1_part * scaled_all, 0)
        else:
            gain_grad1 = jnp.sum(grad_norm1 * (resid_in * inverse1), 0)
        grad_resid = grad_resid + norm_back(resid_in, inverse1, gains[layer, 0], grad_norm1)
        gain_grads[layer] = jnp.stack([gain_grad1, gain_grad2], 0)
        attn_grad = mm("td,trk->rdk", normed_all, grad_mixed) + grad_out
        attn_grad = after(attn_grad, feed_two).astype(bf16)
        attn_grad = halve(attn_grad.reshape(size_row, size_col, 2, half, both), core)
        if layer > 0:
            attn_grad = attn_grad.reshape(size_row * size_col, half, both)
            attn_grads[layer] = exchange_sum(attn_grad, ("row", "col")).astype(bf16)
        else:
            gain_part = jnp.stack(gain_grads, 0)
            gain_part = sum_pairs((gain_part + swap(gain_part, "dp", 1)).astype(bf16))
            gain_rows = gain_part.reshape(-1, both)
            extra = gain_rows.shape[0]
            gain_rows = jnp.pad(gain_rows, ((0, -extra % 8), (0, 0)))
            gain_rows = jnp.broadcast_to(gain_rows, (size_row, size_col) + gain_rows.shape)
            attn_grad = jnp.concatenate([attn_grad, gain_rows], 2)
            attn_grad = scatter_sum(attn_grad, "row").astype(bf16)
            last = attn_grad
            attn_grad = scatter_sum(attn_grad, "col")
            gain_total = attn_grad[half : half + extra].reshape(layers, 2, D)
            attn_grads[layer] = attn_grad[:half].astype(bf16)

    own = [
        jnp.concatenate([attn_grads[layer][None], feed_grads[layer]], 0) for layer in range(layers)
    ]
    own = after(jnp.stack(own, 0), last)
    grads = merge_halves(own, swap(own, "dp", 1), core).astype(f32)
    grads = grads.reshape(layers, 4, deep, both)
    return (
        resid.astype(bf16),
        grad_resid,
        gain_total,
        grads[:, 0, :, :wide_qkv],
        jnp.swapaxes(grads[:, 0, :, wide_qkv:], 1, 2),
        grads[:, 1],
        grads[:, 2],
        jnp.swapaxes(grads[:, 3], 1, 2),
    )


def solution(mesh):
    tokens = P(("dp", "col", "row"), None)
    return jax.shard_map(
        on_device,
        mesh=mesh,
        in_specs=(
            tokens,
            tokens,
            P(("dp", "col")),
            P(),
            P(None, "col", "row"),
            P(None, "row", "col"),
            P(None, "col", "row"),
            P(None, "col", "row"),
            P(None, "row", "col"),
        ),
        out_specs=(
            tokens,
            tokens,
            P(),
            P(None, "col", "row"),
            P(None, "row", "col"),
            P(None, "col", "row"),
            P(None, "col", "row"),
            P(None, "row", "col"),
        ),
        check_vma=False,
    )
```

```python
import jax
import jax.numpy as jnp
from jax import lax
from jax.experimental import pallas as pl
from jax.experimental.pallas import tpu as pltpu
from jax.sharding import PartitionSpec as P

D = 576
HEADS = 9
KV_HEADS = 3
HEAD_DIM = 64
GROUP = HEADS // KV_HEADS
KV = KV_HEADS * HEAD_DIM
QKV = D + 2 * KV

eps_norm = 1e-05
rope_base = 100000.0
masked_score = -1e30
bf16 = jnp.bfloat16
f32 = jnp.float32


def mm(spec, left, right):
    return jnp.einsum(spec, left, right, preferred_element_type=f32)


def rope_tables(token_places):
    half_dim = HEAD_DIM // 2
    places = token_places.astype(f32)
    frequency = rope_base ** (-(2.0 * jnp.arange(half_dim).astype(f32)) / HEAD_DIM)
    angles = places[:, None] * frequency[None, :]
    cosine, sine_vals = jnp.cos(angles), jnp.sin(angles)
    return (
        jnp.concatenate([cosine] * 4, -1),
        jnp.concatenate([-sine_vals, sine_vals] * 2, -1),
    )


def rows_dot(left, right):
    return lax.dot_general(left, right, (((1,), (1,)), ((), ())), preferred_element_type=f32)


def columns_dot(left, right):
    return lax.dot_general(left, right, (((0,), (0,)), ((), ())), preferred_element_type=f32)


def forward_kernel(mixed_ref, cos_ref, sin_ref, bias_ref, att_ref, query_ref, key_ref, lse_ref):
    rows = att_ref.shape[0]
    for chunk in range((D + KV) // 128):
        columns = slice(chunk * 128, chunk * 128 + 128)
        amount = mixed_ref.shape[0] if chunk * 128 + 128 > D else rows
        part = mixed_ref[:amount, columns].astype(f32)
        lane = lax.broadcasted_iota(jnp.int32, part.shape, 1)
        turned = jnp.where(lane % 64 < 32, pltpu.roll(part, 96, 1), pltpu.roll(part, 32, 1))
        part = (part * cos_ref[:amount] + turned * sin_ref[:amount]).astype(bf16)
        if chunk * 128 < D:
            query_ref[:, columns] = part[:rows]
        if chunk * 128 + 128 > D:
            start = chunk * 128 - (D // 128) * 128
            key_ref[:, start : start + 128] = part
    skip = D % 128
    bias = bias_ref[...]
    lses = []
    for group in range(KV_HEADS):
        keys = key_ref[:, skip + group * HEAD_DIM : skip + (group + 1) * HEAD_DIM]
        start = D + KV + group * HEAD_DIM
        values = mixed_ref[:, start : start + HEAD_DIM]
        for head in range(group * GROUP, (group + 1) * GROUP):
            columns = slice(head * HEAD_DIM, (head + 1) * HEAD_DIM)
            scores = rows_dot(query_ref[:, columns], keys) * HEAD_DIM ** (-0.5) + bias
            top = jnp.max(scores, -1, keepdims=True)
            raw = jnp.exp(scores - top)
            total = jnp.sum(raw, -1, keepdims=True)
            probs = (raw * (1.0 / total)).astype(bf16)
            att = jnp.dot(probs, values, preferred_element_type=f32)
            att_ref[:, columns] = att.astype(bf16)
            lses.append(top + jnp.log(total))
    lane = lax.broadcasted_iota(jnp.int32, lse_ref.shape, 1)
    held = jnp.zeros(lse_ref.shape, f32)
    for head in range(HEADS):
        held = jnp.where(lane == head, lses[head], held)
    lse_ref[...] = held


def backward_kernel(
    mixed_ref, query_ref, key_ref, lse_ref, grad_ref, cos_ref, sin_ref, bias_ref, out_ref
):
    rows = query_ref.shape[0]
    block = QKV // out_ref.shape[0]
    scale = HEAD_DIM ** (-0.5)
    out_ref[...] = jnp.zeros(out_ref.shape, bf16)

    def unrotate(part):
        amount = part.shape[0]
        half = HEAD_DIM // 2
        turned = jnp.concatenate([part[:, half:], part[:, :half]], 1)
        return part * cos_ref[:amount, :HEAD_DIM] - turned * sin_ref[:amount, :HEAD_DIM]

    def put(start, part):
        part = part.astype(bf16)
        amount, done = part.shape[0], 0
        while done < HEAD_DIM:
            place, offset = divmod(start + done, block)
            count = min(HEAD_DIM - done, block - offset)
            out_ref[place, :amount, offset : offset + count] = part[:, done : done + count]
            done += count

    skip = D % 128
    bias = bias_ref[...]
    for group in range(KV_HEADS):
        keys = key_ref[:, skip + group * HEAD_DIM : skip + (group + 1) * HEAD_DIM]
        start = D + KV + group * HEAD_DIM
        values = mixed_ref[:, start : start + HEAD_DIM]
        grad_keys, grad_values = None, None
        for head in range(group * GROUP, (group + 1) * GROUP):
            columns = slice(head * HEAD_DIM, (head + 1) * HEAD_DIM)
            query, grad_att = query_ref[:, columns], grad_ref[:, columns]
            scores = rows_dot(query, keys) * scale + bias
            probs = jnp.exp(scores - lse_ref[:, head : head + 1])
            grad_probs = rows_dot(grad_att, values)
            dots = jnp.sum(grad_probs * probs, -1, keepdims=True)
            grad_scores = (probs * (grad_probs - dots)).astype(bf16)
            put(
                head * HEAD_DIM,
                unrotate(jnp.dot(grad_scores, keys, preferred_element_type=f32) * scale),
            )
            for_keys = columns_dot(grad_scores, query)
            for_values = columns_dot(probs.astype(bf16), grad_att)
            grad_keys = for_keys if grad_keys is None else grad_keys + for_keys
            grad_values = for_values if grad_values is None else grad_values + for_values
        put(D + group * HEAD_DIM, unrotate(grad_keys * scale))
        put(D + KV + group * HEAD_DIM, grad_values)


def attend(mixed, cos_wide, sin_wide, bias):
    rows, pack = bias.shape
    return pl.pallas_call(
        forward_kernel,
        out_shape=(
            jax.ShapeDtypeStruct((rows, D), bf16),
            jax.ShapeDtypeStruct((rows, D // 128 * 128 + 128), bf16),
            jax.ShapeDtypeStruct((pack, 256), bf16),
            jax.ShapeDtypeStruct((rows, 128), f32),
        ),
        compiler_params=pltpu.CompilerParams(vmem_limit_bytes=40 * 2**20),
        cost_estimate=pl.CostEstimate(flops=0, bytes_accessed=0, transcendentals=0),
    )(mixed, cos_wide, sin_wide, bias)


def attend_back(mixed, query_rot, keys_rot, lse, grad_att, cos_wide, sin_wide, bias, blocks, wide):
    rows, pack = bias.shape
    return pl.pallas_call(
        backward_kernel,
        out_shape=jax.ShapeDtypeStruct((blocks, pack, wide), bf16),
        compiler_params=pltpu.CompilerParams(vmem_limit_bytes=40 * 2**20),
        cost_estimate=pl.CostEstimate(flops=0, bytes_accessed=0, transcendentals=0),
    )(mixed, query_rot, keys_rot, lse, grad_att, cos_wide, sin_wide, bias)


def norm_back(resid, inverse, gain, grad_norm):
    scaled = resid * inverse
    weighted = grad_norm * gain
    return inverse * (weighted - scaled * jnp.mean(weighted * scaled, -1, keepdims=True))


def swap(values, axis, bit):
    return lax.ppermute(values, axis, [(i, i ^ bit) for i in range(lax.axis_size(axis))])


def neighbours(values, axis):
    return [values] + [swap(values, axis, bits) for bits in range(1, lax.axis_size(axis))]


def in_order(blocks, axis):
    place = lax.axis_index(axis)
    held = jnp.stack(blocks, 0)
    return jnp.stack(
        [
            lax.dynamic_index_in_dim(held, place ^ index, 0, keepdims=False)
            for index in range(len(blocks))
        ],
        0,
    )


def spread(values, axis):
    size = lax.axis_size(axis)
    copies = jnp.broadcast_to(values[None], (size,) + values.shape)
    return lax.all_to_all(copies, axis, 0, 0, tiled=True)


def feed_whole(block, core, size_row, size_col):
    halves = block.reshape(3, 2, block.shape[1] // 2, block.shape[2])
    mine = lax.dynamic_index_in_dim(halves, core, 1, keepdims=False)
    size = lax.axis_size("dp")
    groups = [
        [
            ((2 * pair + data) * size_row + high * 2 + low) * size_col + column
            for high in range(2)
            for column in range(size_col)
            for data in range(2)
        ]
        for pair in range(size // 2)
        for low in range(2)
    ]
    whole = lax.all_gather(mine, ("dp", "row", "col"), axis=0, axis_index_groups=groups)
    return whole.reshape((2, size_col, 2) + mine.shape)


def exchange_sum(values, axes):
    return jnp.sum(lax.all_to_all(values, axes, 0, 0, tiled=True).astype(f32), 0)


def scatter_sum(values, axis):
    place = lax.axis_index(axis)
    total = lax.dynamic_index_in_dim(values, place, 0, keepdims=False).astype(f32)
    for bits in range(1, lax.axis_size(axis)):
        send = lax.dynamic_index_in_dim(values, place ^ bits, 0, keepdims=False)
        total = total + swap(send, axis, bits).astype(f32)
    return total


def after(values, *earlier):
    zero = 0.0
    for array in earlier:
        first = array[(0,) * array.ndim].astype(f32)
        zero = zero + jnp.minimum(jnp.abs(first), 0.0)
    return values + zero.astype(values.dtype)


def merge_halves(own, other, core):
    low = jnp.where(core == 0, own, other)
    high = jnp.where(core == 0, other, own)
    return jnp.stack([low, high], -3)


def joined(part, core):
    whole = merge_halves(part, swap(part, "dp", 1), core)
    return whole.reshape(whole.shape[0], -1, whole.shape[-1])


def sum_pairs(values):
    size = lax.axis_size("dp")
    total = values.astype(f32)
    for step in range(2, size, 2):
        moved = lax.ppermute(values, "dp", [(i, (i + step) % size) for i in range(size)])
        total = total + moved.astype(f32)
    return total.astype(values.dtype)


def halve(values, core):
    axis = values.ndim - 3
    keep = lax.dynamic_index_in_dim(values, core, axis, keepdims=False)
    send = lax.dynamic_index_in_dim(values, 1 - core, axis, keepdims=False)
    return sum_pairs((keep.astype(f32) + swap(send, "dp", 1).astype(f32)).astype(bf16))


def on_device(hidden_in, cotangent, lengths, gains, w_qkv, w_out, w_gate, w_up, w_down):
    rows = hidden_in.shape[0]
    size_row = lax.axis_size("row")
    size_col = lax.axis_size("col")
    core = lax.axis_index("dp") % 2
    pack = rows * size_row
    length = lengths[0]
    layers, deep, wide_qkv = w_qkv.shape
    wide_out = w_out.shape[1]
    wide = w_gate.shape[2]
    half = deep // 2

    both = wide_qkv + wide_out
    attn_blocks = jnp.concatenate([w_qkv, jnp.swapaxes(w_out, 1, 2)], -1)
    attn_half = lax.dynamic_slice_in_dim(attn_blocks, core * half, half, 1)
    feed_blocks = jnp.stack([w_gate, w_up, jnp.swapaxes(w_down, 1, 2)], 1)
    hidden_blocks = neighbours(hidden_in, "row")
    attn_cols = in_order(neighbours(attn_half, "col"), "col")
    attn_parts = spread(after(attn_cols, *hidden_blocks[1:]), "row")
    full_attn = [joined(attn_parts[:, :, 0], core)]
    feed_parts = [feed_whole(feed_blocks[layer], core, size_row, size_col) for layer in range(layers)]
    full_gate, full_up, full_down = [], [], []

    place = lax.axis_index("row")
    key_places = jnp.concatenate(
        [(place ^ bits) * rows + jnp.arange(rows) for bits in range(size_row)], 0
    )
    cosine, sine_vals = rope_tables(key_places)
    query_places = key_places[:rows]
    visible = (key_places[None, :] <= query_places[:, None]) & (key_places[None, :] < length)

    bias = jnp.where(visible, 0.0, masked_score).astype(f32)
    resid = hidden_in.astype(f32)
    late_cotangent = after(cotangent, full_attn[0])
    both_cotangent = jnp.concatenate([cotangent, swap(late_cotangent, "row", 1)], 0)
    stored = []
    for layer in range(layers):
        if layer == 0:
            resid_all = jnp.concatenate(hidden_blocks, 0).astype(f32)
            inverse_all = lax.rsqrt(jnp.mean(resid_all * resid_all, -1, keepdims=True) + eps_norm)
            scaled_all = resid_all * inverse_all
            normed_all = (scaled_all * gains[layer, 0]).astype(bf16)
            inverse1 = inverse_all[:rows]
        else:
            inverse1 = lax.rsqrt(jnp.mean(resid * resid, -1, keepdims=True) + eps_norm)
            normed1 = (resid * inverse1 * gains[layer, 0]).astype(bf16)
            normed_all = jnp.concatenate(neighbours(normed1, "row"), 0)
        mixed = mm("td,rdk->trk", normed_all, full_attn[layer])[:, :, :wide_qkv]
        mixed = mixed.astype(bf16).reshape(pack, QKV)
        attended, query_rot, keys_rot, lse = attend(mixed, cosine, sine_vals, bias)
        attended_blocks = attended.reshape(rows, size_row, wide_out)
        attended_blocks = jnp.pad(attended_blocks, ((0, 0), (0, 0), (wide_qkv, 0)))
        resid_mid = resid + mm("trk,rdk->td", attended_blocks, full_attn[layer])
        inverse2 = lax.rsqrt(jnp.mean(resid_mid * resid_mid, -1, keepdims=True) + eps_norm)
        normed2 = (resid_mid * inverse2 * gains[layer, 1]).astype(bf16)
        both_normed2 = jnp.concatenate([normed2, swap(normed2, "row", 1)], 0)
        feed = after(feed_parts[layer], normed2)
        full_gate.append(feed[:, :, :, 0].reshape(2, D, wide))
        full_up.append(feed[:, :, :, 1].reshape(2, D, wide))
        full_down.append(feed[:, :, :, 2].reshape(2, D, wide))
        gate_act = mm("td,bdf->tbf", both_normed2, full_gate[layer])
        up_act = mm("td,bdf->tbf", both_normed2, full_up[layer])
        hidden = (gate_act * jax.nn.sigmoid(gate_act) * up_act).astype(bf16)
        if layer + 1 < layers:
            full_attn.append(joined(after(attn_parts[:, :, layer + 1], hidden), core))
        down_part = mm("tbf,bdf->td", hidden, full_down[layer])
        moved = swap(down_part[rows:].astype(bf16), "row", 1).astype(f32)
        resid_next = resid_mid + down_part[:rows] + moved
        stored.append(
            (
                resid,
                inverse1,
                normed_all,
                query_rot,
                keys_rot,
                mixed,
                lse,
                attended_blocks,
                resid_mid,
                inverse2,
                both_normed2,
                gate_act,
                up_act,
                hidden,
            )
        )
        resid = resid_next

    grad_resid = cotangent.astype(f32)
    attn_grads = [None] * layers
    feed_grads = [None] * layers
    gain_grads = [None] * layers
    for layer in reversed(range(layers)):
        (
            resid_in,
            inverse1,
            normed_all,
            query_rot,
            keys_rot,
            mixed,
            lse,
            attended_blocks,
            resid_mid,
            inverse2,
            both_normed2,
            gate_act,
            up_act,
            hidden,
        ) = stored[layer]
        if layer == layers - 1:
            both_grad = both_cotangent
        else:
            grad_low = grad_resid.astype(bf16)
            both_grad = jnp.concatenate([grad_low, swap(grad_low, "row", 1)], 0)
        grad_hid = mm("td,bdf->tbf", both_grad, full_down[layer])
        sigma = jax.nn.sigmoid(gate_act)
        grad_gate_act = (grad_hid * up_act * sigma * (1.0 + gate_act * (1.0 - sigma))).astype(bf16)
        grad_up_act = (grad_hid * gate_act * sigma).astype(bf16)
        norm2_part = mm("tbf,bdf->td", grad_gate_act, full_gate[layer])
        norm2_part = norm2_part + mm("tbf,bdf->td", grad_up_act, full_up[layer])
        moved = swap(norm2_part[rows:].astype(bf16), "row", 1).astype(f32)
        grad_norm2 = norm2_part[:rows] + moved
        feed_grad = jnp.stack(
            [
                mm("td,tbf->bdf", both_normed2, grad_gate_act).astype(bf16),
                mm("td,tbf->bdf", both_normed2, grad_up_act).astype(bf16),
                mm("td,tbf->bdf", both_grad, hidden).astype(bf16),
            ],
            1,
        )
        feed_half_sum = halve(feed_grad.reshape(2, 3, size_col, 2, half, wide), core)
        keep = lax.dynamic_index_in_dim(feed_half_sum, place // 2, 0, keepdims=False)
        send = lax.dynamic_index_in_dim(feed_half_sum, 1 - place // 2, 0, keepdims=False)
        feed_two = keep.astype(f32) + swap(send, "row", 2).astype(f32)
        feed_two = jnp.swapaxes(feed_two, 0, 1).astype(bf16).reshape(-1, wide)
        feed_grad = lax.psum_scatter(feed_two, "col", scatter_dimension=0, tiled=True)
        feed_grads[layer] = feed_grad.reshape(3, half, wide)

        gain_grad2 = jnp.sum(grad_norm2 * (resid_mid * inverse2), 0)
        grad_resid = grad_resid + norm_back(resid_mid, inverse2, gains[layer, 1], grad_norm2)
        grad_low = after(grad_resid, feed_half_sum).astype(bf16)
        grad_att = mm("td,rdk->trk", grad_low, full_attn[layer])[:, :, wide_qkv:].astype(bf16)
        grad_att = grad_att.reshape(rows, D)
        grad_out = mm("td,trk->rdk", grad_low, attended_blocks)
        grad_mixed = attend_back(
            mixed, query_rot, keys_rot, lse, grad_att, cosine, sine_vals, bias, size_row, both
        )
        norm1_part = mm("rtk,rdk->td", grad_mixed, full_attn[layer])
        grad_norm1 = norm1_part[:rows]
        norm1_low = norm1_part.astype(bf16)
        for bits in range(1, size_row):
            moved = swap(norm1_low[bits * rows : (bits + 1) * rows], "row", bits)
            grad_norm1 = grad_norm1 + moved.astype(f32)
        if layer == 0:
            gain_grad1 = jnp.sum(norm1_part * scaled_all, 0)
        else:
            gain_grad1 = jnp.sum(grad_norm1 * (resid_in * inverse1), 0)
        grad_resid = grad_resid + norm_back(resid_in, inverse1, gains[layer, 0], grad_norm1)
        gain_grads[layer] = jnp.stack([gain_grad1, gain_grad2], 0)
        attn_grad = mm("td,rtk->rdk", normed_all, grad_mixed) + grad_out
        attn_grad = after(attn_grad, feed_two).astype(bf16)
        attn_grad = halve(attn_grad.reshape(size_row, size_col, 2, half, both), core)
        if layer > 0:
            attn_grad = attn_grad.reshape(size_row * size_col, half, both)
            attn_grads[layer] = exchange_sum(attn_grad, ("row", "col")).astype(bf16)
        else:
            gain_part = jnp.stack(gain_grads, 0)
            gain_part = sum_pairs((gain_part + swap(gain_part, "dp", 1)).astype(bf16))
            gain_rows = gain_part.reshape(-1, both)
            extra = gain_rows.shape[0]
            gain_rows = jnp.pad(gain_rows, ((0, -extra % 8), (0, 0)))
            gain_rows = jnp.broadcast_to(gain_rows, (size_row, size_col) + gain_rows.shape)
            attn_grad = jnp.concatenate([attn_grad, gain_rows], 2)
            attn_grad = scatter_sum(attn_grad, "row").astype(bf16)
            last = attn_grad
            attn_grad = scatter_sum(attn_grad, "col")
            gain_total = attn_grad[half : half + extra].reshape(layers, 2, D)
            attn_grads[layer] = attn_grad[:half].astype(bf16)

    own = [
        jnp.concatenate([attn_grads[layer][None], feed_grads[layer]], 0) for layer in range(layers)
    ]
    own = after(jnp.stack(own, 0), last)
    grads = merge_halves(own, swap(own, "dp", 1), core).astype(f32)
    grads = grads.reshape(layers, 4, deep, both)
    return (
        resid.astype(bf16),
        grad_resid,
        gain_total,
        grads[:, 0, :, :wide_qkv],
        jnp.swapaxes(grads[:, 0, :, wide_qkv:], 1, 2),
        grads[:, 1],
        grads[:, 2],
        jnp.swapaxes(grads[:, 3], 1, 2),
    )


def solution(mesh):
    tokens = P(("dp", "col", "row"), None)
    return jax.shard_map(
        on_device,
        mesh=mesh,
        in_specs=(
            tokens,
            tokens,
            P(("dp", "col")),
            P(),
            P(None, "col", "row"),
            P(None, "row", "col"),
            P(None, "col", "row"),
            P(None, "col", "row"),
            P(None, "row", "col"),
        ),
        out_specs=(
            tokens,
            tokens,
            P(),
            P(None, "col", "row"),
            P(None, "row", "col"),
            P(None, "col", "row"),
            P(None, "col", "row"),
            P(None, "row", "col"),
        ),
        check_vma=False,
    )
```

```python
import jax
import jax.numpy as jnp
from jax import lax
from jax.experimental import pallas as pl
from jax.experimental.pallas import tpu as pltpu
from jax.sharding import PartitionSpec as P

D = 576
HEADS = 9
KV_HEADS = 3
HEAD_DIM = 64
GROUP = HEADS // KV_HEADS
KV = KV_HEADS * HEAD_DIM
QKV = D + 2 * KV

eps_norm = 1e-05
rope_base = 100000.0
masked_score = -1e30
bf16 = jnp.bfloat16
f32 = jnp.float32


def mm(spec, left, right):
    return jnp.einsum(spec, left, right, preferred_element_type=f32)


def rope_tables(token_places):
    half_dim = HEAD_DIM // 2
    places = token_places.astype(f32)
    frequency = rope_base ** (-(2.0 * jnp.arange(half_dim).astype(f32)) / HEAD_DIM)
    angles = places[:, None] * frequency[None, :]
    cosine, sine_vals = jnp.cos(angles), jnp.sin(angles)
    return (
        jnp.concatenate([cosine] * 4, -1),
        jnp.concatenate([-sine_vals, sine_vals] * 2, -1),
    )


def rows_dot(left, right):
    return lax.dot_general(left, right, (((1,), (1,)), ((), ())), preferred_element_type=f32)


def columns_dot(left, right):
    return lax.dot_general(left, right, (((0,), (0,)), ((), ())), preferred_element_type=f32)


def pieces(start, count, block):
    found, done = [], 0
    while done < count:
        place, offset = divmod(start + done, block)
        amount = min(count - done, block - offset)
        found.append((place, offset, amount))
        done += amount
    return found


def take(ref, amount, start, count, block, skip=0):
    parts = [
        ref[place, :amount, skip + offset : skip + offset + size]
        for place, offset, size in pieces(start, count, block)
    ]
    return parts[0] if len(parts) == 1 else jnp.concatenate(parts, 1)


def put(ref, amount, start, part, block, skip=0):
    done = 0
    for place, offset, size in pieces(start, part.shape[1], block):
        ref[place, :amount, skip + offset : skip + offset + size] = part[:, done : done + size]
        done += size


def forward_kernel(mixed_ref, cos_ref, sin_ref, bias_ref, att_ref, query_ref, key_ref, lse_ref):
    blocks, rows, _ = att_ref.shape
    pack = mixed_ref.shape[1]
    wide_qkv, wide_out = QKV // blocks, D // blocks
    att_ref[...] = jnp.zeros(att_ref.shape, bf16)
    for chunk in range((D + KV) // 128):
        columns = slice(chunk * 128, chunk * 128 + 128)
        amount = pack if chunk * 128 + 128 > D else rows
        part = take(mixed_ref, amount, chunk * 128, 128, wide_qkv).astype(f32)
        lane = lax.broadcasted_iota(jnp.int32, part.shape, 1)
        turned = jnp.where(lane % 64 < 32, pltpu.roll(part, 96, 1), pltpu.roll(part, 32, 1))
        part = (part * cos_ref[:amount] + turned * sin_ref[:amount]).astype(bf16)
        if chunk * 128 < D:
            query_ref[:, columns] = part[:rows]
        if chunk * 128 + 128 > D:
            start = chunk * 128 - (D // 128) * 128
            key_ref[:, start : start + 128] = part
    skip = D % 128
    bias = bias_ref[...]
    lses = []
    for group in range(KV_HEADS):
        keys = key_ref[:, skip + group * HEAD_DIM : skip + (group + 1) * HEAD_DIM]
        start = D + KV + group * HEAD_DIM
        values = take(mixed_ref, pack, start, HEAD_DIM, wide_qkv)
        for head in range(group * GROUP, (group + 1) * GROUP):
            columns = slice(head * HEAD_DIM, (head + 1) * HEAD_DIM)
            scores = rows_dot(query_ref[:, columns], keys) * HEAD_DIM ** (-0.5) + bias
            top = jnp.max(scores, -1, keepdims=True)
            raw = jnp.exp(scores - top)
            total = jnp.sum(raw, -1, keepdims=True)
            probs = (raw * (1.0 / total)).astype(bf16)
            att = jnp.dot(probs, values, preferred_element_type=f32)
            put(att_ref, rows, head * HEAD_DIM, att.astype(bf16), wide_out, wide_qkv)
            lses.append(top + jnp.log(total))
    lane = lax.broadcasted_iota(jnp.int32, lse_ref.shape, 1)
    held = jnp.zeros(lse_ref.shape, f32)
    for head in range(HEADS):
        held = jnp.where(lane == head, lses[head], held)
    lse_ref[...] = held


def backward_kernel(
    mixed_ref, query_ref, key_ref, lse_ref, grad_ref, cos_ref, sin_ref, bias_ref, out_ref
):
    rows = query_ref.shape[0]
    blocks, pack, _ = out_ref.shape
    wide_qkv, wide_out = QKV // blocks, D // blocks
    scale = HEAD_DIM ** (-0.5)
    out_ref[...] = jnp.zeros(out_ref.shape, bf16)

    def unrotate(part):
        amount = part.shape[0]
        half = HEAD_DIM // 2
        turned = jnp.concatenate([part[:, half:], part[:, :half]], 1)
        return part * cos_ref[:amount, :HEAD_DIM] - turned * sin_ref[:amount, :HEAD_DIM]

    skip = D % 128
    bias = bias_ref[...]
    for group in range(KV_HEADS):
        keys = key_ref[:, skip + group * HEAD_DIM : skip + (group + 1) * HEAD_DIM]
        start = D + KV + group * HEAD_DIM
        values = take(mixed_ref, pack, start, HEAD_DIM, wide_qkv)
        grad_keys, grad_values = None, None
        for head in range(group * GROUP, (group + 1) * GROUP):
            columns = slice(head * HEAD_DIM, (head + 1) * HEAD_DIM)
            query = query_ref[:, columns]
            grad_att = take(grad_ref, rows, head * HEAD_DIM, HEAD_DIM, wide_out, wide_qkv)
            scores = rows_dot(query, keys) * scale + bias
            probs = jnp.exp(scores - lse_ref[:, head : head + 1])
            grad_probs = rows_dot(grad_att, values)
            dots = jnp.sum(grad_probs * probs, -1, keepdims=True)
            grad_scores = (probs * (grad_probs - dots)).astype(bf16)
            grad_query = jnp.dot(grad_scores, keys, preferred_element_type=f32) * scale
            grad_query = unrotate(grad_query).astype(bf16)
            put(out_ref, rows, head * HEAD_DIM, grad_query, wide_qkv)
            for_keys = columns_dot(grad_scores, query)
            for_values = columns_dot(probs.astype(bf16), grad_att)
            grad_keys = for_keys if grad_keys is None else grad_keys + for_keys
            grad_values = for_values if grad_values is None else grad_values + for_values
        grad_keys = unrotate(grad_keys * scale).astype(bf16)
        put(out_ref, pack, D + group * HEAD_DIM, grad_keys, wide_qkv)
        put(out_ref, pack, start, grad_values.astype(bf16), wide_qkv)


def attend(mixed, cos_wide, sin_wide, bias):
    rows, pack = bias.shape
    return pl.pallas_call(
        forward_kernel,
        out_shape=(
            jax.ShapeDtypeStruct((mixed.shape[0], rows, mixed.shape[2]), bf16),
            jax.ShapeDtypeStruct((rows, D // 128 * 128 + 128), bf16),
            jax.ShapeDtypeStruct((pack, 256), bf16),
            jax.ShapeDtypeStruct((rows, 128), f32),
        ),
        compiler_params=pltpu.CompilerParams(vmem_limit_bytes=40 * 2**20),
        cost_estimate=pl.CostEstimate(flops=0, bytes_accessed=0, transcendentals=0),
    )(mixed, cos_wide, sin_wide, bias)


def attend_back(mixed, query_rot, keys_rot, lse, grad_att, cos_wide, sin_wide, bias):
    rows, pack = bias.shape
    return pl.pallas_call(
        backward_kernel,
        out_shape=jax.ShapeDtypeStruct(mixed.shape, bf16),
        compiler_params=pltpu.CompilerParams(vmem_limit_bytes=40 * 2**20),
        cost_estimate=pl.CostEstimate(flops=0, bytes_accessed=0, transcendentals=0),
    )(mixed, query_rot, keys_rot, lse, grad_att, cos_wide, sin_wide, bias)


def norm_back(resid, inverse, gain, grad_norm):
    scaled = resid * inverse
    weighted = grad_norm * gain
    return inverse * (weighted - scaled * jnp.mean(weighted * scaled, -1, keepdims=True))


def swap(values, axis, bit):
    return lax.ppermute(values, axis, [(i, i ^ bit) for i in range(lax.axis_size(axis))])


def neighbours(values, axis):
    return [values] + [swap(values, axis, bits) for bits in range(1, lax.axis_size(axis))]


def in_order(blocks, axis):
    place = lax.axis_index(axis)
    held = jnp.stack(blocks, 0)
    return jnp.stack(
        [
            lax.dynamic_index_in_dim(held, place ^ index, 0, keepdims=False)
            for index in range(len(blocks))
        ],
        0,
    )


def spread(values, axis):
    size = lax.axis_size(axis)
    copies = jnp.broadcast_to(values[None], (size,) + values.shape)
    return lax.all_to_all(copies, axis, 0, 0, tiled=True)


def feed_whole(block, core, size_row, size_col):
    halves = block.reshape(3, 2, block.shape[1] // 2, block.shape[2])
    mine = lax.dynamic_index_in_dim(halves, core, 1, keepdims=False)
    size = lax.axis_size("dp")
    groups = [
        [
            ((2 * pair + data) * size_row + high * 2 + low) * size_col + column
            for high in range(2)
            for column in range(size_col)
            for data in range(2)
        ]
        for pair in range(size // 2)
        for low in range(2)
    ]
    whole = lax.all_gather(mine, ("dp", "row", "col"), axis=0, axis_index_groups=groups)
    return whole.reshape((2, size_col, 2) + mine.shape)


def exchange_sum(values, axes):
    return jnp.sum(lax.all_to_all(values, axes, 0, 0, tiled=True).astype(f32), 0)


def scatter_sum(values, axis):
    place = lax.axis_index(axis)
    total = lax.dynamic_index_in_dim(values, place, 0, keepdims=False).astype(f32)
    for bits in range(1, lax.axis_size(axis)):
        send = lax.dynamic_index_in_dim(values, place ^ bits, 0, keepdims=False)
        total = total + swap(send, axis, bits).astype(f32)
    return total


def after(values, *earlier):
    zero = 0.0
    for array in earlier:
        first = array[(0,) * array.ndim].astype(f32)
        zero = zero + jnp.minimum(jnp.abs(first), 0.0)
    return values + zero.astype(values.dtype)


def merge_halves(own, other, core):
    low = jnp.where(core == 0, own, other)
    high = jnp.where(core == 0, other, own)
    return jnp.stack([low, high], -3)


def joined(part, core):
    whole = merge_halves(part, swap(part, "dp", 1), core)
    return whole.reshape(whole.shape[0], -1, whole.shape[-1])


def sum_pairs(values):
    size = lax.axis_size("dp")
    total = values.astype(f32)
    for step in range(2, size, 2):
        moved = lax.ppermute(values, "dp", [(i, (i + step) % size) for i in range(size)])
        total = total + moved.astype(f32)
    return total.astype(values.dtype)


def halve(values, core):
    axis = values.ndim - 3
    keep = lax.dynamic_index_in_dim(values, core, axis, keepdims=False)
    send = lax.dynamic_index_in_dim(values, 1 - core, axis, keepdims=False)
    return sum_pairs((keep.astype(f32) + swap(send, "dp", 1).astype(f32)).astype(bf16))


def on_device(hidden_in, cotangent, lengths, gains, w_qkv, w_out, w_gate, w_up, w_down):
    rows = hidden_in.shape[0]
    size_row = lax.axis_size("row")
    size_col = lax.axis_size("col")
    core = lax.axis_index("dp") % 2
    pack = rows * size_row
    length = lengths[0]
    layers, deep, wide_qkv = w_qkv.shape
    wide_out = w_out.shape[1]
    wide = w_gate.shape[2]
    half = deep // 2

    both = wide_qkv + wide_out
    attn_blocks = jnp.concatenate([w_qkv, jnp.swapaxes(w_out, 1, 2)], -1)
    attn_half = lax.dynamic_slice_in_dim(attn_blocks, core * half, half, 1)
    feed_blocks = jnp.stack([w_gate, w_up, jnp.swapaxes(w_down, 1, 2)], 1)
    hidden_blocks = neighbours(hidden_in, "row")
    attn_cols = in_order(neighbours(attn_half, "col"), "col")
    attn_parts = spread(after(attn_cols, *hidden_blocks[1:]), "row")
    full_attn = [joined(attn_parts[:, :, 0], core)]
    feed_parts = [feed_whole(feed_blocks[layer], core, size_row, size_col) for layer in range(layers)]
    full_gate, full_up, full_down = [], [], []

    place = lax.axis_index("row")
    key_places = jnp.concatenate(
        [(place ^ bits) * rows + jnp.arange(rows) for bits in range(size_row)], 0
    )
    cosine, sine_vals = rope_tables(key_places)
    query_places = key_places[:rows]
    visible = (key_places[None, :] <= query_places[:, None]) & (key_places[None, :] < length)

    bias = jnp.where(visible, 0.0, masked_score).astype(f32)
    resid = hidden_in.astype(f32)
    late_cotangent = after(cotangent, full_attn[0])
    both_cotangent = jnp.concatenate([cotangent, swap(late_cotangent, "row", 1)], 0)
    stored = []
    for layer in range(layers):
        if layer == 0:
            resid_all = jnp.concatenate(hidden_blocks, 0).astype(f32)
            inverse_all = lax.rsqrt(jnp.mean(resid_all * resid_all, -1, keepdims=True) + eps_norm)
            scaled_all = resid_all * inverse_all
            normed_all = (scaled_all * gains[layer, 0]).astype(bf16)
            inverse1 = inverse_all[:rows]
        else:
            inverse1 = lax.rsqrt(jnp.mean(resid * resid, -1, keepdims=True) + eps_norm)
            normed1 = (resid * inverse1 * gains[layer, 0]).astype(bf16)
            normed_all = jnp.concatenate(neighbours(normed1, "row"), 0)
        mixed = mm("td,rdk->rtk", normed_all, full_attn[layer]).astype(bf16)
        attended_blocks, query_rot, keys_rot, lse = attend(mixed, cosine, sine_vals, bias)
        resid_mid = resid + mm("rtk,rdk->td", attended_blocks, full_attn[layer])
        inverse2 = lax.rsqrt(jnp.mean(resid_mid * resid_mid, -1, keepdims=True) + eps_norm)
        normed2 = (resid_mid * inverse2 * gains[layer, 1]).astype(bf16)
        both_normed2 = jnp.concatenate([normed2, swap(normed2, "row", 1)], 0)
        feed = after(feed_parts[layer], normed2)
        full_gate.append(feed[:, :, :, 0].reshape(2, D, wide))
        full_up.append(feed[:, :, :, 1].reshape(2, D, wide))
        full_down.append(feed[:, :, :, 2].reshape(2, D, wide))
        gate_act = mm("td,bdf->tbf", both_normed2, full_gate[layer])
        up_act = mm("td,bdf->tbf", both_normed2, full_up[layer])
        hidden = (gate_act * jax.nn.sigmoid(gate_act) * up_act).astype(bf16)
        if layer + 1 < layers:
            full_attn.append(joined(after(attn_parts[:, :, layer + 1], hidden), core))
        down_part = mm("tbf,bdf->td", hidden, full_down[layer])
        moved = swap(down_part[rows:].astype(bf16), "row", 1).astype(f32)
        resid_next = resid_mid + down_part[:rows] + moved
        stored.append(
            (
                resid,
                inverse1,
                normed_all,
                query_rot,
                keys_rot,
                mixed,
                lse,
                attended_blocks,
                resid_mid,
                inverse2,
                both_normed2,
                gate_act,
                up_act,
                hidden,
            )
        )
        resid = resid_next

    grad_resid = cotangent.astype(f32)
    attn_grads = [None] * layers
    feed_grads = [None] * layers
    gain_grads = [None] * layers
    for layer in reversed(range(layers)):
        (
            resid_in,
            inverse1,
            normed_all,
            query_rot,
            keys_rot,
            mixed,
            lse,
            attended_blocks,
            resid_mid,
            inverse2,
            both_normed2,
            gate_act,
            up_act,
            hidden,
        ) = stored[layer]
        if layer == layers - 1:
            both_grad = both_cotangent
        else:
            grad_low = grad_resid.astype(bf16)
            both_grad = jnp.concatenate([grad_low, swap(grad_low, "row", 1)], 0)
        grad_hid = mm("td,bdf->tbf", both_grad, full_down[layer])
        sigma = jax.nn.sigmoid(gate_act)
        grad_gate_act = (grad_hid * up_act * sigma * (1.0 + gate_act * (1.0 - sigma))).astype(bf16)
        grad_up_act = (grad_hid * gate_act * sigma).astype(bf16)
        norm2_part = mm("tbf,bdf->td", grad_gate_act, full_gate[layer])
        norm2_part = norm2_part + mm("tbf,bdf->td", grad_up_act, full_up[layer])
        moved = swap(norm2_part[rows:].astype(bf16), "row", 1).astype(f32)
        grad_norm2 = norm2_part[:rows] + moved
        feed_grad = jnp.stack(
            [
                mm("td,tbf->bdf", both_normed2, grad_gate_act).astype(bf16),
                mm("td,tbf->bdf", both_normed2, grad_up_act).astype(bf16),
                mm("td,tbf->bdf", both_grad, hidden).astype(bf16),
            ],
            1,
        )
        feed_half_sum = halve(feed_grad.reshape(2, 3, size_col, 2, half, wide), core)
        keep = lax.dynamic_index_in_dim(feed_half_sum, place // 2, 0, keepdims=False)
        send = lax.dynamic_index_in_dim(feed_half_sum, 1 - place // 2, 0, keepdims=False)
        feed_two = keep.astype(f32) + swap(send, "row", 2).astype(f32)
        feed_two = jnp.swapaxes(feed_two, 0, 1).astype(bf16).reshape(-1, wide)
        feed_grad = lax.psum_scatter(feed_two, "col", scatter_dimension=0, tiled=True)
        feed_grads[layer] = feed_grad.reshape(3, half, wide)

        gain_grad2 = jnp.sum(grad_norm2 * (resid_mid * inverse2), 0)
        grad_resid = grad_resid + norm_back(resid_mid, inverse2, gains[layer, 1], grad_norm2)
        grad_low = after(grad_resid, feed_half_sum).astype(bf16)
        grad_att = mm("td,rdk->rtk", grad_low, full_attn[layer]).astype(bf16)
        grad_out = mm("td,rtk->rdk", grad_low, attended_blocks)
        grad_mixed = attend_back(
            mixed, query_rot, keys_rot, lse, grad_att, cosine, sine_vals, bias
        )
        norm1_part = mm("rtk,rdk->td", grad_mixed, full_attn[layer])
        grad_norm1 = norm1_part[:rows]
        norm1_low = norm1_part.astype(bf16)
        for bits in range(1, size_row):
            moved = swap(norm1_low[bits * rows : (bits + 1) * rows], "row", bits)
            grad_norm1 = grad_norm1 + moved.astype(f32)
        if layer == 0:
            gain_grad1 = jnp.sum(norm1_part * scaled_all, 0)
        else:
            gain_grad1 = jnp.sum(grad_norm1 * (resid_in * inverse1), 0)
        grad_resid = grad_resid + norm_back(resid_in, inverse1, gains[layer, 0], grad_norm1)
        gain_grads[layer] = jnp.stack([gain_grad1, gain_grad2], 0)
        attn_grad = mm("td,rtk->rdk", normed_all, grad_mixed) + grad_out
        attn_grad = after(attn_grad, feed_two).astype(bf16)
        attn_grad = halve(attn_grad.reshape(size_row, size_col, 2, half, both), core)
        if layer > 0:
            attn_grad = attn_grad.reshape(size_row * size_col, half, both)
            attn_grads[layer] = exchange_sum(attn_grad, ("row", "col")).astype(bf16)
        else:
            gain_part = jnp.stack(gain_grads, 0)
            gain_part = sum_pairs((gain_part + swap(gain_part, "dp", 1)).astype(bf16))
            gain_rows = gain_part.reshape(-1, both)
            extra = gain_rows.shape[0]
            gain_rows = jnp.pad(gain_rows, ((0, -extra % 8), (0, 0)))
            gain_rows = jnp.broadcast_to(gain_rows, (size_row, size_col) + gain_rows.shape)
            attn_grad = jnp.concatenate([attn_grad, gain_rows], 2)
            attn_grad = scatter_sum(attn_grad, "row").astype(bf16)
            last = attn_grad
            attn_grad = scatter_sum(attn_grad, "col")
            gain_total = attn_grad[half : half + extra].reshape(layers, 2, D)
            attn_grads[layer] = attn_grad[:half].astype(bf16)

    own = [
        jnp.concatenate([attn_grads[layer][None], feed_grads[layer]], 0) for layer in range(layers)
    ]
    own = after(jnp.stack(own, 0), last)
    grads = merge_halves(own, swap(own, "dp", 1), core).astype(f32)
    grads = grads.reshape(layers, 4, deep, both)
    return (
        resid.astype(bf16),
        grad_resid,
        gain_total,
        grads[:, 0, :, :wide_qkv],
        jnp.swapaxes(grads[:, 0, :, wide_qkv:], 1, 2),
        grads[:, 1],
        grads[:, 2],
        jnp.swapaxes(grads[:, 3], 1, 2),
    )


def solution(mesh):
    tokens = P(("dp", "col", "row"), None)
    return jax.shard_map(
        on_device,
        mesh=mesh,
        in_specs=(
            tokens,
            tokens,
            P(("dp", "col")),
            P(),
            P(None, "col", "row"),
            P(None, "row", "col"),
            P(None, "col", "row"),
            P(None, "col", "row"),
            P(None, "row", "col"),
        ),
        out_specs=(
            tokens,
            tokens,
            P(),
            P(None, "col", "row"),
            P(None, "row", "col"),
            P(None, "col", "row"),
            P(None, "col", "row"),
            P(None, "row", "col"),
        ),
        check_vma=False,
    )
```

```python
import jax
import jax.numpy as jnp
from jax import lax
from jax.experimental import pallas as pl
from jax.experimental.pallas import tpu as pltpu
from jax.sharding import PartitionSpec as P

D = 576
HEADS = 9
KV_HEADS = 3
HEAD_DIM = 64
GROUP = HEADS // KV_HEADS
KV = KV_HEADS * HEAD_DIM
QKV = D + 2 * KV

eps_norm = 1e-05
rope_base = 100000.0
masked_score = -1e30
bf16 = jnp.bfloat16
f32 = jnp.float32


def mm(spec, left, right):
    return jnp.einsum(spec, left, right, preferred_element_type=f32)


def rope_tables(token_places):
    half_dim = HEAD_DIM // 2
    places = token_places.astype(f32)
    frequency = rope_base ** (-(2.0 * jnp.arange(half_dim).astype(f32)) / HEAD_DIM)
    angles = places[:, None] * frequency[None, :]
    cosine, sine_vals = jnp.cos(angles), jnp.sin(angles)
    return (
        jnp.concatenate([cosine] * 4, -1),
        jnp.concatenate([-sine_vals, sine_vals] * 2, -1),
    )


def rows_dot(left, right):
    return lax.dot_general(left, right, (((1,), (1,)), ((), ())), preferred_element_type=f32)


def columns_dot(left, right):
    return lax.dot_general(left, right, (((0,), (0,)), ((), ())), preferred_element_type=f32)


def pieces(start, count, block):
    found, done = [], 0
    while done < count:
        place, offset = divmod(start + done, block)
        amount = min(count - done, block - offset)
        found.append((place, offset, amount))
        done += amount
    return found


def take(ref, amount, start, count, block, skip=0):
    parts = [
        ref[place, :amount, skip + offset : skip + offset + size]
        for place, offset, size in pieces(start, count, block)
    ]
    return parts[0] if len(parts) == 1 else jnp.concatenate(parts, 1)


def put(ref, amount, start, part, block, skip=0):
    done = 0
    for place, offset, size in pieces(start, part.shape[1], block):
        ref[place, :amount, skip + offset : skip + offset + size] = part[:, done : done + size]
        done += size


def forward_kernel(mixed_ref, cos_ref, sin_ref, bias_ref, att_ref, query_ref, key_ref, lse_ref):
    blocks, rows, _ = att_ref.shape
    pack = mixed_ref.shape[1]
    wide_qkv, wide_out = QKV // blocks, D // blocks
    att_ref[...] = jnp.zeros(att_ref.shape, bf16)
    for chunk in range((D + KV) // 128):
        columns = slice(chunk * 128, chunk * 128 + 128)
        amount = pack if chunk * 128 + 128 > D else rows
        part = take(mixed_ref, amount, chunk * 128, 128, wide_qkv).astype(f32)
        lane = lax.broadcasted_iota(jnp.int32, part.shape, 1)
        turned = jnp.where(lane % 64 < 32, pltpu.roll(part, 96, 1), pltpu.roll(part, 32, 1))
        part = (part * cos_ref[:amount] + turned * sin_ref[:amount]).astype(bf16)
        if chunk * 128 < D:
            query_ref[:, columns] = part[:rows]
        if chunk * 128 + 128 > D:
            start = chunk * 128 - (D // 128) * 128
            key_ref[:, start : start + 128] = part
    skip = D % 128
    bias = bias_ref[...]
    lses = []
    for group in range(KV_HEADS):
        keys = key_ref[:, skip + group * HEAD_DIM : skip + (group + 1) * HEAD_DIM]
        start = D + KV + group * HEAD_DIM
        values = take(mixed_ref, pack, start, HEAD_DIM, wide_qkv)
        for head in range(group * GROUP, (group + 1) * GROUP):
            columns = slice(head * HEAD_DIM, (head + 1) * HEAD_DIM)
            scores = rows_dot(query_ref[:, columns], keys) * HEAD_DIM ** (-0.5) + bias
            top = jnp.max(scores, -1, keepdims=True)
            raw = jnp.exp(scores - top)
            total = jnp.sum(raw, -1, keepdims=True)
            probs = (raw * (1.0 / total)).astype(bf16)
            att = jnp.dot(probs, values, preferred_element_type=f32)
            put(att_ref, rows, head * HEAD_DIM, att.astype(bf16), wide_out, wide_qkv)
            lses.append(top + jnp.log(total))
    lane = lax.broadcasted_iota(jnp.int32, lse_ref.shape, 1)
    held = jnp.zeros(lse_ref.shape, f32)
    for head in range(HEADS):
        held = jnp.where(lane == head, lses[head], held)
    lse_ref[...] = held


def backward_kernel(
    mixed_ref, query_ref, key_ref, lse_ref, grad_ref, cos_ref, sin_ref, bias_ref, out_ref
):
    rows = query_ref.shape[0]
    blocks, pack, _ = out_ref.shape
    wide_qkv, wide_out = QKV // blocks, D // blocks
    scale = HEAD_DIM ** (-0.5)
    out_ref[...] = jnp.zeros(out_ref.shape, bf16)

    def unrotate(part):
        amount = part.shape[0]
        half = HEAD_DIM // 2
        turned = jnp.concatenate([part[:, half:], part[:, :half]], 1)
        return part * cos_ref[:amount, :HEAD_DIM] - turned * sin_ref[:amount, :HEAD_DIM]

    skip = D % 128
    bias = bias_ref[...]
    for group in range(KV_HEADS):
        keys = key_ref[:, skip + group * HEAD_DIM : skip + (group + 1) * HEAD_DIM]
        start = D + KV + group * HEAD_DIM
        values = take(mixed_ref, pack, start, HEAD_DIM, wide_qkv)
        grad_keys, grad_values = None, None
        for head in range(group * GROUP, (group + 1) * GROUP):
            columns = slice(head * HEAD_DIM, (head + 1) * HEAD_DIM)
            query = query_ref[:, columns]
            grad_att = take(grad_ref, rows, head * HEAD_DIM, HEAD_DIM, wide_out, wide_qkv)
            scores = rows_dot(query, keys) * scale + bias
            probs = jnp.exp(scores - lse_ref[:, head : head + 1])
            grad_probs = rows_dot(grad_att, values)
            dots = jnp.sum(grad_probs * probs, -1, keepdims=True)
            grad_scores = (probs * (grad_probs - dots)).astype(bf16)
            grad_query = jnp.dot(grad_scores, keys, preferred_element_type=f32) * scale
            grad_query = unrotate(grad_query).astype(bf16)
            put(out_ref, rows, head * HEAD_DIM, grad_query, wide_qkv)
            for_keys = columns_dot(grad_scores, query)
            for_values = columns_dot(probs.astype(bf16), grad_att)
            grad_keys = for_keys if grad_keys is None else grad_keys + for_keys
            grad_values = for_values if grad_values is None else grad_values + for_values
        grad_keys = unrotate(grad_keys * scale).astype(bf16)
        put(out_ref, pack, D + group * HEAD_DIM, grad_keys, wide_qkv)
        put(out_ref, pack, start, grad_values.astype(bf16), wide_qkv)


def attend(mixed, cos_wide, sin_wide, bias):
    rows, pack = bias.shape
    return pl.pallas_call(
        forward_kernel,
        out_shape=(
            jax.ShapeDtypeStruct((mixed.shape[0], rows, mixed.shape[2]), bf16),
            jax.ShapeDtypeStruct((rows, D // 128 * 128 + 128), bf16),
            jax.ShapeDtypeStruct((pack, 256), bf16),
            jax.ShapeDtypeStruct((rows, 128), f32),
        ),
        compiler_params=pltpu.CompilerParams(vmem_limit_bytes=40 * 2**20),
        cost_estimate=pl.CostEstimate(flops=0, bytes_accessed=0, transcendentals=0),
    )(mixed, cos_wide, sin_wide, bias)


def attend_back(mixed, query_rot, keys_rot, lse, grad_att, cos_wide, sin_wide, bias):
    rows, pack = bias.shape
    return pl.pallas_call(
        backward_kernel,
        out_shape=jax.ShapeDtypeStruct(mixed.shape, bf16),
        compiler_params=pltpu.CompilerParams(vmem_limit_bytes=40 * 2**20),
        cost_estimate=pl.CostEstimate(flops=0, bytes_accessed=0, transcendentals=0),
    )(mixed, query_rot, keys_rot, lse, grad_att, cos_wide, sin_wide, bias)


def norm_back(resid, inverse, gain, grad_norm):
    scaled = resid * inverse
    weighted = grad_norm * gain
    return inverse * (weighted - scaled * jnp.mean(weighted * scaled, -1, keepdims=True))


def swap(values, axis, bit):
    return lax.ppermute(values, axis, [(i, i ^ bit) for i in range(lax.axis_size(axis))])


def neighbours(values, axis):
    return [values] + [swap(values, axis, bits) for bits in range(1, lax.axis_size(axis))]


def in_order(blocks, axis):
    place = lax.axis_index(axis)
    held = jnp.stack(blocks, 0)
    return jnp.stack(
        [
            lax.dynamic_index_in_dim(held, place ^ index, 0, keepdims=False)
            for index in range(len(blocks))
        ],
        0,
    )


def spread(values, axis):
    size = lax.axis_size(axis)
    copies = jnp.broadcast_to(values[None], (size,) + values.shape)
    return lax.all_to_all(copies, axis, 0, 0, tiled=True)


def feed_whole(block, core, size_row, size_col):
    halves = block.reshape(3, 2, block.shape[1] // 2, block.shape[2])
    mine = lax.dynamic_index_in_dim(halves, core, 1, keepdims=False)
    size = lax.axis_size("dp")
    groups = [
        [
            ((2 * pair + data) * size_row + high * 2 + low) * size_col + column
            for high in range(2)
            for column in range(size_col)
            for data in range(2)
        ]
        for pair in range(size // 2)
        for low in range(2)
    ]
    whole = lax.all_gather(mine, ("dp", "row", "col"), axis=0, axis_index_groups=groups)
    return whole.reshape((2, size_col, 2) + mine.shape)


def exchange_sum(values, axes):
    return jnp.sum(lax.all_to_all(values, axes, 0, 0, tiled=True).astype(f32), 0)


def scatter_sum(values, axis):
    place = lax.axis_index(axis)
    total = lax.dynamic_index_in_dim(values, place, 0, keepdims=False).astype(f32)
    for bits in range(1, lax.axis_size(axis)):
        send = lax.dynamic_index_in_dim(values, place ^ bits, 0, keepdims=False)
        total = total + swap(send, axis, bits).astype(f32)
    return total


def after(values, *earlier):
    zero = 0.0
    for array in earlier:
        first = array[(0,) * array.ndim].astype(f32)
        zero = zero + jnp.minimum(jnp.abs(first), 0.0)
    return values + zero.astype(values.dtype)


def merge_halves(own, other, core):
    low = jnp.where(core == 0, own, other)
    high = jnp.where(core == 0, other, own)
    return jnp.stack([low, high], -3)


def joined(part, core):
    whole = merge_halves(part, swap(part, "dp", 1), core)
    return whole.reshape(whole.shape[0], -1, whole.shape[-1])


def sum_pairs(values):
    size = lax.axis_size("dp")
    total = values.astype(f32)
    for step in range(2, size, 2):
        moved = lax.ppermute(values, "dp", [(i, (i + step) % size) for i in range(size)])
        total = total + moved.astype(f32)
    return total.astype(values.dtype)


def halve(values, core):
    axis = values.ndim - 3
    keep = lax.dynamic_index_in_dim(values, core, axis, keepdims=False)
    send = lax.dynamic_index_in_dim(values, 1 - core, axis, keepdims=False)
    return sum_pairs((keep.astype(f32) + swap(send, "dp", 1).astype(f32)).astype(bf16))


def on_device(hidden_in, cotangent, lengths, gains, w_qkv, w_out, w_gate, w_up, w_down):
    rows = hidden_in.shape[0]
    size_row = lax.axis_size("row")
    size_col = lax.axis_size("col")
    core = lax.axis_index("dp") % 2
    pack = rows * size_row
    length = lengths[0]
    layers, deep, wide_qkv = w_qkv.shape
    wide_out = w_out.shape[1]
    wide = w_gate.shape[2]
    half = deep // 2

    both = wide_qkv + wide_out
    attn_blocks = jnp.concatenate([w_qkv, jnp.swapaxes(w_out, 1, 2)], -1)
    attn_half = lax.dynamic_slice_in_dim(attn_blocks, core * half, half, 1)
    feed_blocks = jnp.stack([w_gate, w_up, jnp.swapaxes(w_down, 1, 2)], 1)
    hidden_blocks = neighbours(hidden_in, "row")
    attn_cols = in_order(neighbours(attn_half, "col"), "col")
    attn_parts = spread(after(attn_cols, hidden_blocks[3]), "row")
    full_attn = [joined(attn_parts[:, :, 0], core)]
    feed_parts = [feed_whole(feed_blocks[layer], core, size_row, size_col) for layer in range(layers)]
    full_gate, full_up, full_down = [], [], []

    place = lax.axis_index("row")
    key_places = jnp.concatenate(
        [(place ^ bits) * rows + jnp.arange(rows) for bits in range(size_row)], 0
    )
    cosine, sine_vals = rope_tables(key_places)
    query_places = key_places[:rows]
    visible = (key_places[None, :] <= query_places[:, None]) & (key_places[None, :] < length)

    bias = jnp.where(visible, 0.0, masked_score).astype(f32)
    resid = hidden_in.astype(f32)
    late_cotangent = after(cotangent, full_attn[0])
    both_cotangent = jnp.concatenate([cotangent, swap(late_cotangent, "row", 1)], 0)
    stored = []
    for layer in range(layers):
        if layer == 0:
            resid_all = jnp.concatenate(hidden_blocks, 0).astype(f32)
            inverse_all = lax.rsqrt(jnp.mean(resid_all * resid_all, -1, keepdims=True) + eps_norm)
            scaled_all = resid_all * inverse_all
            normed_all = (scaled_all * gains[layer, 0]).astype(bf16)
            inverse1 = inverse_all[:rows]
        else:
            inverse1 = lax.rsqrt(jnp.mean(resid * resid, -1, keepdims=True) + eps_norm)
            normed1 = (resid * inverse1 * gains[layer, 0]).astype(bf16)
            normed_all = jnp.concatenate(neighbours(normed1, "row"), 0)
        mixed = mm("td,rdk->rtk", normed_all, full_attn[layer]).astype(bf16)
        attended_blocks, query_rot, keys_rot, lse = attend(mixed, cosine, sine_vals, bias)
        resid_mid = resid + mm("rtk,rdk->td", attended_blocks, full_attn[layer])
        inverse2 = lax.rsqrt(jnp.mean(resid_mid * resid_mid, -1, keepdims=True) + eps_norm)
        normed2 = (resid_mid * inverse2 * gains[layer, 1]).astype(bf16)
        both_normed2 = jnp.concatenate([normed2, swap(normed2, "row", 1)], 0)
        feed = after(feed_parts[layer], normed2)
        full_gate.append(feed[:, :, :, 0].reshape(2, D, wide))
        full_up.append(feed[:, :, :, 1].reshape(2, D, wide))
        full_down.append(feed[:, :, :, 2].reshape(2, D, wide))
        gate_act = mm("td,bdf->tbf", both_normed2, full_gate[layer])
        up_act = mm("td,bdf->tbf", both_normed2, full_up[layer])
        hidden = (gate_act * jax.nn.sigmoid(gate_act) * up_act).astype(bf16)
        if layer + 1 < layers:
            full_attn.append(joined(after(attn_parts[:, :, layer + 1], hidden), core))
        down_part = mm("tbf,bdf->td", hidden, full_down[layer])
        moved = swap(down_part[rows:].astype(bf16), "row", 1).astype(f32)
        resid_next = resid_mid + down_part[:rows] + moved
        stored.append(
            (
                resid,
                inverse1,
                normed_all,
                query_rot,
                keys_rot,
                mixed,
                lse,
                attended_blocks,
                resid_mid,
                inverse2,
                both_normed2,
                gate_act,
                up_act,
                hidden,
            )
        )
        resid = resid_next

    grad_resid = cotangent.astype(f32)
    attn_grads = [None] * layers
    feed_grads = [None] * layers
    gain_grads = [None] * layers
    for layer in reversed(range(layers)):
        (
            resid_in,
            inverse1,
            normed_all,
            query_rot,
            keys_rot,
            mixed,
            lse,
            attended_blocks,
            resid_mid,
            inverse2,
            both_normed2,
            gate_act,
            up_act,
            hidden,
        ) = stored[layer]
        if layer == layers - 1:
            both_grad = both_cotangent
        else:
            grad_low = grad_resid.astype(bf16)
            both_grad = jnp.concatenate([grad_low, swap(grad_low, "row", 1)], 0)
        grad_hid = mm("td,bdf->tbf", both_grad, full_down[layer])
        sigma = jax.nn.sigmoid(gate_act)
        grad_gate_act = (grad_hid * up_act * sigma * (1.0 + gate_act * (1.0 - sigma))).astype(bf16)
        grad_up_act = (grad_hid * gate_act * sigma).astype(bf16)
        norm2_part = mm("tbf,bdf->td", grad_gate_act, full_gate[layer])
        norm2_part = norm2_part + mm("tbf,bdf->td", grad_up_act, full_up[layer])
        moved = swap(norm2_part[rows:].astype(bf16), "row", 1).astype(f32)
        grad_norm2 = norm2_part[:rows] + moved
        feed_grad = jnp.stack(
            [
                mm("td,tbf->bdf", both_normed2, grad_gate_act).astype(bf16),
                mm("td,tbf->bdf", both_normed2, grad_up_act).astype(bf16),
                mm("td,tbf->bdf", both_grad, hidden).astype(bf16),
            ],
            1,
        )
        feed_half_sum = halve(feed_grad.reshape(2, 3, size_col, 2, half, wide), core)
        keep = lax.dynamic_index_in_dim(feed_half_sum, place // 2, 0, keepdims=False)
        send = lax.dynamic_index_in_dim(feed_half_sum, 1 - place // 2, 0, keepdims=False)
        feed_two = keep.astype(f32) + swap(send, "row", 2).astype(f32)
        feed_two = jnp.swapaxes(feed_two, 0, 1).astype(bf16).reshape(-1, wide)
        feed_grad = lax.psum_scatter(feed_two, "col", scatter_dimension=0, tiled=True)
        feed_grads[layer] = feed_grad.reshape(3, half, wide)

        gain_grad2 = jnp.sum(grad_norm2 * (resid_mid * inverse2), 0)
        grad_resid = grad_resid + norm_back(resid_mid, inverse2, gains[layer, 1], grad_norm2)
        grad_low = grad_resid if layer > 0 else after(grad_resid, feed_half_sum)
        grad_low = grad_low.astype(bf16)
        grad_att = mm("td,rdk->rtk", grad_low, full_attn[layer]).astype(bf16)
        grad_out = mm("td,rtk->rdk", grad_low, attended_blocks)
        grad_mixed = attend_back(
            mixed, query_rot, keys_rot, lse, grad_att, cosine, sine_vals, bias
        )
        norm1_part = mm("rtk,rdk->td", grad_mixed, full_attn[layer])
        grad_norm1 = norm1_part[:rows]
        norm1_low = norm1_part.astype(bf16)
        for bits in range(1, size_row):
            moved = swap(norm1_low[bits * rows : (bits + 1) * rows], "row", bits)
            grad_norm1 = grad_norm1 + moved.astype(f32)
        if layer == 0:
            gain_grad1 = jnp.sum(norm1_part * scaled_all, 0)
        else:
            gain_grad1 = jnp.sum(grad_norm1 * (resid_in * inverse1), 0)
        grad_resid = grad_resid + norm_back(resid_in, inverse1, gains[layer, 0], grad_norm1)
        gain_grads[layer] = jnp.stack([gain_grad1, gain_grad2], 0)
        attn_grad = mm("td,rtk->rdk", normed_all, grad_mixed) + grad_out
        attn_grad = after(attn_grad, feed_two).astype(bf16)
        attn_grad = halve(attn_grad.reshape(size_row, size_col, 2, half, both), core)
        if layer > 0:
            attn_grad = attn_grad.reshape(size_row * size_col, half, both)
            attn_grads[layer] = exchange_sum(attn_grad, ("row", "col")).astype(bf16)
        else:
            gain_part = jnp.stack(gain_grads, 0)
            gain_part = sum_pairs((gain_part + swap(gain_part, "dp", 1)).astype(bf16))
            gain_rows = gain_part.reshape(-1, both)
            extra = gain_rows.shape[0]
            gain_rows = jnp.pad(gain_rows, ((0, -extra % 8), (0, 0)))
            gain_rows = jnp.broadcast_to(gain_rows, (size_row, size_col) + gain_rows.shape)
            attn_grad = jnp.concatenate([attn_grad, gain_rows], 2)
            attn_grad = scatter_sum(attn_grad, "row").astype(bf16)
            last = attn_grad
            attn_grad = scatter_sum(attn_grad, "col")
            gain_total = attn_grad[half : half + extra].reshape(layers, 2, D)
            attn_grads[layer] = attn_grad[:half].astype(bf16)

    own = [
        jnp.concatenate([attn_grads[layer][None], feed_grads[layer]], 0) for layer in range(layers)
    ]
    own = after(jnp.stack(own, 0), last)
    grads = merge_halves(own, swap(own, "dp", 1), core).astype(f32)
    grads = grads.reshape(layers, 4, deep, both)
    return (
        resid.astype(bf16),
        grad_resid,
        gain_total,
        grads[:, 0, :, :wide_qkv],
        jnp.swapaxes(grads[:, 0, :, wide_qkv:], 1, 2),
        grads[:, 1],
        grads[:, 2],
        jnp.swapaxes(grads[:, 3], 1, 2),
    )


def solution(mesh):
    tokens = P(("dp", "col", "row"), None)
    return jax.shard_map(
        on_device,
        mesh=mesh,
        in_specs=(
            tokens,
            tokens,
            P(("dp", "col")),
            P(),
            P(None, "col", "row"),
            P(None, "row", "col"),
            P(None, "col", "row"),
            P(None, "col", "row"),
            P(None, "row", "col"),
        ),
        out_specs=(
            tokens,
            tokens,
            P(),
            P(None, "col", "row"),
            P(None, "row", "col"),
            P(None, "col", "row"),
            P(None, "col", "row"),
            P(None, "row", "col"),
        ),
        check_vma=False,
    )
```

```python
import jax
import jax.numpy as jnp
from jax import lax
from jax.experimental import pallas as pl
from jax.experimental.pallas import tpu as pltpu
from jax.sharding import PartitionSpec as P

D = 576
HEADS = 9
KV_HEADS = 3
HEAD_DIM = 64
GROUP = HEADS // KV_HEADS
KV = KV_HEADS * HEAD_DIM
QKV = D + 2 * KV

eps_norm = 1e-05
rope_base = 100000.0
masked_score = -1e30
bf16 = jnp.bfloat16
f32 = jnp.float32


def mm(spec, left, right):
    return jnp.einsum(spec, left, right, preferred_element_type=f32)


def rope_tables(token_places):
    half_dim = HEAD_DIM // 2
    places = token_places.astype(f32)
    frequency = rope_base ** (-(2.0 * jnp.arange(half_dim).astype(f32)) / HEAD_DIM)
    angles = places[:, None] * frequency[None, :]
    cosine, sine_vals = jnp.cos(angles), jnp.sin(angles)
    return (
        jnp.concatenate([cosine] * 4, -1),
        jnp.concatenate([-sine_vals, sine_vals] * 2, -1),
    )


def rows_dot(left, right):
    return lax.dot_general(left, right, (((1,), (1,)), ((), ())), preferred_element_type=f32)


def columns_dot(left, right):
    return lax.dot_general(left, right, (((0,), (0,)), ((), ())), preferred_element_type=f32)


def pieces(start, count, block):
    found, done = [], 0
    while done < count:
        place, offset = divmod(start + done, block)
        amount = min(count - done, block - offset)
        found.append((place, offset, amount))
        done += amount
    return found


def take(ref, amount, start, count, block, skip=0):
    parts = [
        ref[place, :amount, skip + offset : skip + offset + size]
        for place, offset, size in pieces(start, count, block)
    ]
    return parts[0] if len(parts) == 1 else jnp.concatenate(parts, 1)


def put(ref, amount, start, part, block, skip=0):
    done = 0
    for place, offset, size in pieces(start, part.shape[1], block):
        ref[place, :amount, skip + offset : skip + offset + size] = part[:, done : done + size]
        done += size


def forward_kernel(mixed_ref, cos_ref, sin_ref, bias_ref, att_ref, query_ref, key_ref, lse_ref):
    blocks, rows, _ = att_ref.shape
    pack = mixed_ref.shape[1]
    wide_qkv, wide_out = QKV // blocks, D // blocks
    att_ref[...] = jnp.zeros(att_ref.shape, bf16)
    for chunk in range((D + KV) // 128):
        columns = slice(chunk * 128, chunk * 128 + 128)
        amount = pack if chunk * 128 + 128 > D else rows
        part = take(mixed_ref, amount, chunk * 128, 128, wide_qkv).astype(f32)
        lane = lax.broadcasted_iota(jnp.int32, part.shape, 1)
        turned = jnp.where(lane % 64 < 32, pltpu.roll(part, 96, 1), pltpu.roll(part, 32, 1))
        part = (part * cos_ref[:amount] + turned * sin_ref[:amount]).astype(bf16)
        if chunk * 128 < D:
            query_ref[:, columns] = part[:rows]
        if chunk * 128 + 128 > D:
            start = chunk * 128 - (D // 128) * 128
            key_ref[:, start : start + 128] = part
    skip = D % 128
    bias = bias_ref[...]
    lses = []
    for group in range(KV_HEADS):
        keys = key_ref[:, skip + group * HEAD_DIM : skip + (group + 1) * HEAD_DIM]
        start = D + KV + group * HEAD_DIM
        values = take(mixed_ref, pack, start, HEAD_DIM, wide_qkv)
        for head in range(group * GROUP, (group + 1) * GROUP):
            columns = slice(head * HEAD_DIM, (head + 1) * HEAD_DIM)
            scores = rows_dot(query_ref[:, columns], keys) * HEAD_DIM ** (-0.5) + bias
            top = jnp.max(scores, -1, keepdims=True)
            raw = jnp.exp(scores - top)
            total = jnp.sum(raw, -1, keepdims=True)
            probs = (raw * (1.0 / total)).astype(bf16)
            att = jnp.dot(probs, values, preferred_element_type=f32)
            put(att_ref, rows, head * HEAD_DIM, att.astype(bf16), wide_out, wide_qkv)
            lses.append(top + jnp.log(total))
    lane = lax.broadcasted_iota(jnp.int32, lse_ref.shape, 1)
    held = jnp.zeros(lse_ref.shape, f32)
    for head in range(HEADS):
        held = jnp.where(lane == head, lses[head], held)
    lse_ref[...] = held


def backward_kernel(
    mixed_ref, query_ref, key_ref, lse_ref, grad_ref, cos_ref, sin_ref, bias_ref, out_ref
):
    rows = query_ref.shape[0]
    blocks, pack, _ = out_ref.shape
    wide_qkv, wide_out = QKV // blocks, D // blocks
    scale = HEAD_DIM ** (-0.5)
    out_ref[...] = jnp.zeros(out_ref.shape, bf16)

    def unrotate(part):
        amount = part.shape[0]
        half = HEAD_DIM // 2
        turned = jnp.concatenate([part[:, half:], part[:, :half]], 1)
        return part * cos_ref[:amount, :HEAD_DIM] - turned * sin_ref[:amount, :HEAD_DIM]

    skip = D % 128
    bias = bias_ref[...]
    for group in range(KV_HEADS):
        keys = key_ref[:, skip + group * HEAD_DIM : skip + (group + 1) * HEAD_DIM]
        start = D + KV + group * HEAD_DIM
        values = take(mixed_ref, pack, start, HEAD_DIM, wide_qkv)
        grad_keys, grad_values = None, None
        for head in range(group * GROUP, (group + 1) * GROUP):
            columns = slice(head * HEAD_DIM, (head + 1) * HEAD_DIM)
            query = query_ref[:, columns]
            grad_att = take(grad_ref, rows, head * HEAD_DIM, HEAD_DIM, wide_out, wide_qkv)
            scores = rows_dot(query, keys) * scale + bias
            probs = jnp.exp(scores - lse_ref[:, head : head + 1])
            grad_probs = rows_dot(grad_att, values)
            dots = jnp.sum(grad_probs * probs, -1, keepdims=True)
            grad_scores = (probs * (grad_probs - dots)).astype(bf16)
            grad_query = jnp.dot(grad_scores, keys, preferred_element_type=f32) * scale
            grad_query = unrotate(grad_query).astype(bf16)
            put(out_ref, rows, head * HEAD_DIM, grad_query, wide_qkv)
            for_keys = columns_dot(grad_scores, query)
            for_values = columns_dot(probs.astype(bf16), grad_att)
            grad_keys = for_keys if grad_keys is None else grad_keys + for_keys
            grad_values = for_values if grad_values is None else grad_values + for_values
        grad_keys = unrotate(grad_keys * scale).astype(bf16)
        put(out_ref, pack, D + group * HEAD_DIM, grad_keys, wide_qkv)
        put(out_ref, pack, start, grad_values.astype(bf16), wide_qkv)


def attend(mixed, cos_wide, sin_wide, bias):
    rows, pack = bias.shape
    return pl.pallas_call(
        forward_kernel,
        out_shape=(
            jax.ShapeDtypeStruct((mixed.shape[0], rows, mixed.shape[2]), bf16),
            jax.ShapeDtypeStruct((rows, D // 128 * 128 + 128), bf16),
            jax.ShapeDtypeStruct((pack, 256), bf16),
            jax.ShapeDtypeStruct((rows, 128), f32),
        ),
        compiler_params=pltpu.CompilerParams(vmem_limit_bytes=40 * 2**20),
        cost_estimate=pl.CostEstimate(flops=0, bytes_accessed=0, transcendentals=0),
    )(mixed, cos_wide, sin_wide, bias)


def attend_back(mixed, query_rot, keys_rot, lse, grad_att, cos_wide, sin_wide, bias):
    rows, pack = bias.shape
    return pl.pallas_call(
        backward_kernel,
        out_shape=jax.ShapeDtypeStruct(mixed.shape, bf16),
        compiler_params=pltpu.CompilerParams(vmem_limit_bytes=40 * 2**20),
        cost_estimate=pl.CostEstimate(flops=0, bytes_accessed=0, transcendentals=0),
    )(mixed, query_rot, keys_rot, lse, grad_att, cos_wide, sin_wide, bias)


def norm_back(resid, inverse, gain, grad_norm):
    scaled = resid * inverse
    weighted = grad_norm * gain
    return inverse * (weighted - scaled * jnp.mean(weighted * scaled, -1, keepdims=True))


def swap(values, axis, bit):
    return lax.ppermute(values, axis, [(i, i ^ bit) for i in range(lax.axis_size(axis))])


def neighbours(values, axis):
    return [values] + [swap(values, axis, bits) for bits in range(1, lax.axis_size(axis))]


def in_order(blocks, axis):
    place = lax.axis_index(axis)
    held = jnp.stack(blocks, 0)
    return jnp.stack(
        [
            lax.dynamic_index_in_dim(held, place ^ index, 0, keepdims=False)
            for index in range(len(blocks))
        ],
        0,
    )


def spread(values, axis):
    size = lax.axis_size(axis)
    copies = jnp.broadcast_to(values[None], (size,) + values.shape)
    return lax.all_to_all(copies, axis, 0, 0, tiled=True)


def feed_whole(block, core, size_row, size_col):
    halves = block.reshape(3, 2, block.shape[1] // 2, block.shape[2])
    mine = lax.dynamic_index_in_dim(halves, core, 1, keepdims=False)
    size = lax.axis_size("dp")
    groups = [
        [
            ((2 * pair + data) * size_row + high * 2 + low) * size_col + column
            for high in range(2)
            for column in range(size_col)
            for data in range(2)
        ]
        for pair in range(size // 2)
        for low in range(2)
    ]
    whole = lax.all_gather(mine, ("dp", "row", "col"), axis=0, axis_index_groups=groups)
    return whole.reshape((2, size_col, 2) + mine.shape)


def exchange_sum(values, axes):
    return jnp.sum(lax.all_to_all(values, axes, 0, 0, tiled=True).astype(f32), 0)


def scatter_sum(values, axis):
    place = lax.axis_index(axis)
    total = lax.dynamic_index_in_dim(values, place, 0, keepdims=False).astype(f32)
    for bits in range(1, lax.axis_size(axis)):
        send = lax.dynamic_index_in_dim(values, place ^ bits, 0, keepdims=False)
        total = total + swap(send, axis, bits).astype(f32)
    return total


def after(values, *earlier):
    zero = 0.0
    for array in earlier:
        first = array[(0,) * array.ndim].astype(f32)
        zero = zero + jnp.minimum(jnp.abs(first), 0.0)
    return values + zero.astype(values.dtype)


def merge_halves(own, other, core):
    low = jnp.where(core == 0, own, other)
    high = jnp.where(core == 0, other, own)
    return jnp.stack([low, high], -3)


def joined(part, core):
    whole = merge_halves(part, swap(part, "dp", 1), core)
    return whole.reshape(whole.shape[0], -1, whole.shape[-1])


def sum_pairs(values):
    size = lax.axis_size("dp")
    total = values.astype(f32)
    for step in range(2, size, 2):
        moved = lax.ppermute(values, "dp", [(i, (i + step) % size) for i in range(size)])
        total = total + moved.astype(f32)
    return total.astype(values.dtype)


def halve(values, core):
    axis = values.ndim - 3
    keep = lax.dynamic_index_in_dim(values, core, axis, keepdims=False)
    send = lax.dynamic_index_in_dim(values, 1 - core, axis, keepdims=False)
    return sum_pairs((keep.astype(f32) + swap(send, "dp", 1).astype(f32)).astype(bf16))


def on_device(hidden_in, cotangent, lengths, gains, w_qkv, w_out, w_gate, w_up, w_down):
    rows = hidden_in.shape[0]
    size_row = lax.axis_size("row")
    size_col = lax.axis_size("col")
    core = lax.axis_index("dp") % 2
    pack = rows * size_row
    length = lengths[0]
    layers, deep, wide_qkv = w_qkv.shape
    wide_out = w_out.shape[1]
    wide = w_gate.shape[2]
    half = deep // 2

    both = wide_qkv + wide_out
    attn_blocks = jnp.concatenate([w_qkv, jnp.swapaxes(w_out, 1, 2)], -1)
    attn_half = lax.dynamic_slice_in_dim(attn_blocks, core * half, half, 1)
    feed_blocks = jnp.stack([w_gate, w_up, jnp.swapaxes(w_down, 1, 2)], 1)
    hidden_blocks = neighbours(hidden_in, "row")
    attn_cols = in_order(neighbours(attn_half, "col"), "col")
    attn_parts = spread(after(attn_cols, hidden_blocks[3]), "row")
    full_attn = [joined(attn_parts[:, :, 0], core)]
    feed_parts = [feed_whole(feed_blocks[layer], core, size_row, size_col) for layer in range(layers)]
    full_gate, full_up, full_down = [], [], []

    place = lax.axis_index("row")
    key_places = jnp.concatenate(
        [(place ^ bits) * rows + jnp.arange(rows) for bits in range(size_row)], 0
    )
    cosine, sine_vals = rope_tables(key_places)
    query_places = key_places[:rows]
    visible = (key_places[None, :] <= query_places[:, None]) & (key_places[None, :] < length)

    bias = jnp.where(visible, 0.0, masked_score).astype(f32)
    resid = hidden_in.astype(f32)
    late_cotangent = after(cotangent, full_attn[0])
    both_cotangent = jnp.concatenate([cotangent, swap(late_cotangent, "row", 1)], 0)
    stored = []
    for layer in range(layers):
        if layer == 0:
            resid_all = jnp.concatenate(hidden_blocks, 0).astype(f32)
            inverse_all = lax.rsqrt(jnp.mean(resid_all * resid_all, -1, keepdims=True) + eps_norm)
            scaled_all = resid_all * inverse_all
            normed_all = (scaled_all * gains[layer, 0]).astype(bf16)
            inverse1 = inverse_all[:rows]
        else:
            inverse1 = lax.rsqrt(jnp.mean(resid * resid, -1, keepdims=True) + eps_norm)
            normed1 = (resid * inverse1 * gains[layer, 0]).astype(bf16)
            normed_all = jnp.concatenate(neighbours(normed1, "row"), 0)
        mixed = mm("td,rdk->rtk", normed_all, full_attn[layer]).astype(bf16)
        attended_blocks, query_rot, keys_rot, lse = attend(mixed, cosine, sine_vals, bias)
        resid_mid = resid + mm("rtk,rdk->td", attended_blocks, full_attn[layer])
        inverse2 = lax.rsqrt(jnp.mean(resid_mid * resid_mid, -1, keepdims=True) + eps_norm)
        normed2 = (resid_mid * inverse2 * gains[layer, 1]).astype(bf16)
        both_normed2 = jnp.concatenate([normed2, swap(normed2, "row", 1)], 0)
        feed = feed_parts[layer] if layer == 0 else after(feed_parts[layer], normed2)
        full_gate.append(feed[:, :, :, 0].reshape(2, D, wide))
        full_up.append(feed[:, :, :, 1].reshape(2, D, wide))
        full_down.append(feed[:, :, :, 2].reshape(2, D, wide))
        gate_act = mm("td,bdf->tbf", both_normed2, full_gate[layer])
        up_act = mm("td,bdf->tbf", both_normed2, full_up[layer])
        hidden = (gate_act * jax.nn.sigmoid(gate_act) * up_act).astype(bf16)
        if layer + 1 < layers:
            full_attn.append(joined(after(attn_parts[:, :, layer + 1], hidden), core))
        down_part = mm("tbf,bdf->td", hidden, full_down[layer])
        moved = swap(down_part[rows:].astype(bf16), "row", 1).astype(f32)
        resid_next = resid_mid + down_part[:rows] + moved
        stored.append(
            (
                resid,
                inverse1,
                normed_all,
                query_rot,
                keys_rot,
                mixed,
                lse,
                attended_blocks,
                resid_mid,
                inverse2,
                both_normed2,
                gate_act,
                up_act,
                hidden,
            )
        )
        resid = resid_next

    grad_resid = cotangent.astype(f32)
    attn_grads = [None] * layers
    feed_grads = [None] * layers
    gain_grads = [None] * layers
    for layer in reversed(range(layers)):
        (
            resid_in,
            inverse1,
            normed_all,
            query_rot,
            keys_rot,
            mixed,
            lse,
            attended_blocks,
            resid_mid,
            inverse2,
            both_normed2,
            gate_act,
            up_act,
            hidden,
        ) = stored[layer]
        if layer == layers - 1:
            both_grad = both_cotangent
        else:
            grad_low = grad_resid.astype(bf16)
            both_grad = jnp.concatenate([grad_low, swap(grad_low, "row", 1)], 0)
        grad_hid = mm("td,bdf->tbf", both_grad, full_down[layer])
        sigma = jax.nn.sigmoid(gate_act)
        grad_gate_act = (grad_hid * up_act * sigma * (1.0 + gate_act * (1.0 - sigma))).astype(bf16)
        grad_up_act = (grad_hid * gate_act * sigma).astype(bf16)
        norm2_part = mm("tbf,bdf->td", grad_gate_act, full_gate[layer])
        norm2_part = norm2_part + mm("tbf,bdf->td", grad_up_act, full_up[layer])
        moved = swap(norm2_part[rows:].astype(bf16), "row", 1).astype(f32)
        grad_norm2 = norm2_part[:rows] + moved
        feed_grad = jnp.stack(
            [
                mm("td,tbf->bdf", both_normed2, grad_gate_act).astype(bf16),
                mm("td,tbf->bdf", both_normed2, grad_up_act).astype(bf16),
                mm("td,tbf->bdf", both_grad, hidden).astype(bf16),
            ],
            1,
        )
        feed_half_sum = halve(feed_grad.reshape(2, 3, size_col, 2, half, wide), core)
        keep = lax.dynamic_index_in_dim(feed_half_sum, place // 2, 0, keepdims=False)
        send = lax.dynamic_index_in_dim(feed_half_sum, 1 - place // 2, 0, keepdims=False)
        feed_two = keep.astype(f32) + swap(send, "row", 2).astype(f32)
        feed_two = jnp.swapaxes(feed_two, 0, 1).astype(bf16).reshape(-1, wide)
        feed_grad = lax.psum_scatter(feed_two, "col", scatter_dimension=0, tiled=True)
        feed_grads[layer] = feed_grad.reshape(3, half, wide)

        gain_grad2 = jnp.sum(grad_norm2 * (resid_mid * inverse2), 0)
        grad_resid = grad_resid + norm_back(resid_mid, inverse2, gains[layer, 1], grad_norm2)
        grad_low = grad_resid if layer > 0 else after(grad_resid, feed_half_sum)
        grad_low = grad_low.astype(bf16)
        grad_att = mm("td,rdk->rtk", grad_low, full_attn[layer]).astype(bf16)
        grad_out = mm("td,rtk->rdk", grad_low, attended_blocks)
        grad_mixed = attend_back(
            mixed, query_rot, keys_rot, lse, grad_att, cosine, sine_vals, bias
        )
        norm1_part = mm("rtk,rdk->td", grad_mixed, full_attn[layer])
        grad_norm1 = norm1_part[:rows]
        norm1_low = norm1_part.astype(bf16)
        for bits in range(1, size_row):
            moved = swap(norm1_low[bits * rows : (bits + 1) * rows], "row", bits)
            grad_norm1 = grad_norm1 + moved.astype(f32)
        if layer == 0:
            gain_grad1 = jnp.sum(norm1_part * scaled_all, 0)
        else:
            gain_grad1 = jnp.sum(grad_norm1 * (resid_in * inverse1), 0)
        grad_resid = grad_resid + norm_back(resid_in, inverse1, gains[layer, 0], grad_norm1)
        gain_grads[layer] = jnp.stack([gain_grad1, gain_grad2], 0)
        attn_grad = mm("td,rtk->rdk", normed_all, grad_mixed) + grad_out
        attn_grad = after(attn_grad, feed_two).astype(bf16)
        attn_grad = halve(attn_grad.reshape(size_row, size_col, 2, half, both), core)
        if layer > 0:
            attn_grad = attn_grad.reshape(size_row * size_col, half, both)
            attn_grads[layer] = exchange_sum(attn_grad, ("row", "col")).astype(bf16)
        else:
            gain_part = jnp.stack(gain_grads, 0)
            gain_part = sum_pairs((gain_part + swap(gain_part, "dp", 1)).astype(bf16))
            gain_rows = gain_part.reshape(-1, both)
            extra = gain_rows.shape[0]
            gain_rows = jnp.pad(gain_rows, ((0, -extra % 8), (0, 0)))
            gain_rows = jnp.broadcast_to(gain_rows, (size_row, size_col) + gain_rows.shape)
            attn_grad = jnp.concatenate([attn_grad, gain_rows], 2)
            attn_grad = scatter_sum(attn_grad, "row").astype(bf16)
            last = attn_grad
            attn_grad = scatter_sum(attn_grad, "col")
            gain_total = attn_grad[half : half + extra].reshape(layers, 2, D)
            attn_grads[layer] = attn_grad[:half].astype(bf16)

    own = [
        jnp.concatenate([attn_grads[layer][None], feed_grads[layer]], 0) for layer in range(layers)
    ]
    own = after(jnp.stack(own, 0), last)
    grads = merge_halves(own, swap(own, "dp", 1), core).astype(f32)
    grads = grads.reshape(layers, 4, deep, both)
    return (
        resid.astype(bf16),
        grad_resid,
        gain_total,
        grads[:, 0, :, :wide_qkv],
        jnp.swapaxes(grads[:, 0, :, wide_qkv:], 1, 2),
        grads[:, 1],
        grads[:, 2],
        jnp.swapaxes(grads[:, 3], 1, 2),
    )


def solution(mesh):
    tokens = P(("dp", "col", "row"), None)
    return jax.shard_map(
        on_device,
        mesh=mesh,
        in_specs=(
            tokens,
            tokens,
            P(("dp", "col")),
            P(),
            P(None, "col", "row"),
            P(None, "row", "col"),
            P(None, "col", "row"),
            P(None, "col", "row"),
            P(None, "row", "col"),
        ),
        out_specs=(
            tokens,
            tokens,
            P(),
            P(None, "col", "row"),
            P(None, "row", "col"),
            P(None, "col", "row"),
            P(None, "col", "row"),
            P(None, "row", "col"),
        ),
        check_vma=False,
    )
```
